128 devices in a mesh: row: 16 (over y_lo, x, core), col: 8 (over y_hi, z).
Axes of the slice: x: 4, y: 4 (y_hi: 2, y_lo: 2; y = y_hi * 2 + y_lo), z: 4, core: 2. Of those that a mesh axis runs over, the one named last changes fastest.
Arguments:
- child_factor: float32 [4, 16, 256, 1024], P(None, 'row', None, 'col'), may hold values from -1 to 1
- parent: float32 [4, 16, 256, 8, 8, 256], P(None, 'row', None, None, 'col'), may hold values from -6 to 6
- row_map: int32 [2, 32, 256], replicated, may hold values from 0 to 255, each once within a row
- child_listed: int32 [2, 32, 32], replicated, may hold values 0 or 1
- inv_diag: float32 [512, 512], replicated, as said below
- panel_listed: int32 [64, 64], replicated, may hold values 0 or 1
Outputs:
- factored: float32 [4, 16, 256, 8, 8, 256], P(None, 'row', None, None, 'col')
- panel_factor: float32 [4, 16, 256, 512], P(None, 'row')
The draws below stay inside these ranges and needn't reach their ends.
Inputs may be any that keep to these rules, and one draw needn't show every extreme that they name: `row_map`: for every child and block, the 256 entries are a permutation of 0 to 255. `inv_diag`: lower triangular with a positive diagonal.
All inputs are finite; a program needn't handle non-finite values.
Results may differ from the reference program's by a relative error of at most 0.0001.
Values sent between devices are 32-bit elements; how exact they have to be, the bound alone decides.
No kernel may reach another device: no remote copies, remote signals or barrier semaphores. Data moves between devices by JAX's collectives and lax.ppermute only.
A program may use at most 128 MiB of HBM per device.

```python
import math
import jax
import jax.numpy as jnp
from jax import lax

BS = 256
NC = 8192
KC = 1024
NP = 16384
PW = 512
SHIFT = 16
NCB = 32
NB = 64
NBS = 4
LBR = 4
LBC = 8
N_ROW = 16
N_COL = 8


def draw_inv_diag(key, part):
    key = jax.random.fold_in(key, 5)
    first_key, second_key = jax.random.split(key)
    row_ids = jnp.arange(PW)[:, None]
    col_ids = jnp.arange(PW)[None, :]
    diagonal = jnp.exp(jax.random.uniform(first_key, (PW, 1), jnp.float32, math.log(0.1), math.log(0.3)))
    spread = 0.12 * (row_ids.astype(jnp.float32) + 1.0) ** (-0.5)
    lower_part = jax.random.normal(second_key, (PW, PW), jnp.float32) * spread
    return jnp.where(row_ids > col_ids, lower_part, jnp.where(row_ids == col_ids, diagonal, 0.0)).astype(jnp.float32)


def touch_ends(drawn, key, least, top_value):
    longest = drawn.shape.index(max(drawn.shape))
    spots = []
    for shift in (0, 1):
        where = [jax.random.randint(jax.random.fold_in(key, axis), (), 0, length) for axis, length in enumerate(drawn.shape)]
        where[longest] = (where[longest] + shift) % drawn.shape[longest]
        spots.append(tuple(where))
    return drawn.at[spots[0]].set(least).at[spots[1]].set(top_value)


def shard_levels(own_key, extent, cuts, smallest, high):
    gain = 1.0
    for dim, shards_of in cuts:
        steps = jax.random.uniform(jax.random.fold_in(jax.random.fold_in(own_key, 6), dim), (shards_of,), jnp.float32, smallest / len(cuts), high / len(cuts))
        gain = gain * jnp.repeat(jnp.exp(steps), extent[dim] // shards_of).reshape((-1,) + (1,) * (len(extent) - 1 - dim))
    return gain


def scatter_about(rng, shape, scale, reach, shards=(), kind=jnp.bfloat16):
    loudness = shard_levels(rng, shape, shards, -0.22, 0.18) if shards else 1.0
    result = jax.random.normal(rng, shape, jnp.float32) * scale * loudness
    return jnp.minimum(jnp.maximum(result, -reach), reach).astype(kind)


def setup_inputs(seed: int = 0) -> dict:
    streams_of = jax.random.split(jax.random.key(seed), 7)
    child_factor = scatter_about(streams_of[0], (NBS, N_ROW, BS, KC), 0.18, 1.0, ((1, 16), (3, 8)), jnp.float32)
    parent = scatter_about(streams_of[1], (LBR, N_ROW, BS, LBC, N_COL, BS), 1.0, 6.0, ((1, 16), (4, 8)), jnp.float32)
    row_map = jax.vmap(lambda own: jax.random.permutation(own, BS))(jax.random.split(streams_of[2], 2 * NCB)).reshape((2, NCB, BS)).astype(jnp.int32)
    child_listed = touch_ends((jax.random.randint(streams_of[3], (2, NCB, NCB), 0, 4) < 3).astype(jnp.int32), jax.random.fold_in(streams_of[3], 1), 0, 1)
    inv_diag = draw_inv_diag(jax.random.fold_in(streams_of[6], 71), 0)
    panel_listed = touch_ends((jax.random.randint(streams_of[5], (NB, NB), 0, 4) < 3).astype(jnp.int32), jax.random.fold_in(streams_of[5], 1), 0, 1)
    return {"child_factor": child_factor, "parent": parent, "row_map": row_map, "child_listed": child_listed, "inv_diag": inv_diag, "panel_listed": panel_listed}


def reference(child_factor, parent, row_map, child_listed, inv_diag, panel_listed):
    precise = lax.Precision.HIGHEST
    half_rows = N_ROW // 2
    child_blocks = NC // BS
    slab_count = child_blocks // half_rows
    parent_blocks = NP // BS
    assembled = parent.reshape(NP, NP)
    factors = child_factor.reshape(slab_count, 2, half_rows, BS, KC).transpose(1, 0, 2, 3, 4).reshape(2, NC, KC)
    for child_index in range(2):
        update = jnp.dot(factors[child_index], factors[child_index].T, precision=precise, preferred_element_type=jnp.float32)
        block_mask = jnp.repeat(jnp.repeat(child_listed[child_index].astype(jnp.float32), BS, axis=0), BS, axis=1)
        targets = ((jnp.arange(child_blocks, dtype=jnp.int32)[:, None] + SHIFT * child_index) * BS + row_map[child_index]).reshape(NC).astype(jnp.int32)
        assembled = assembled.at[targets[:, None], targets[None, :]].add(-(update * block_mask))
    panel_rows = jnp.dot(assembled[:, :PW], inv_diag.T, precision=precise, preferred_element_type=jnp.float32)
    blocks = jnp.arange(parent_blocks)
    trailing = (blocks[:, None] >= PW // BS) & (blocks[None, :] >= PW // BS) & (panel_listed == 1)
    product = jnp.dot(panel_rows, panel_rows.T, precision=precise, preferred_element_type=jnp.float32).reshape(parent_blocks, BS, parent_blocks, BS)
    factored = assembled.reshape(parent_blocks, BS, parent_blocks, BS) - jnp.where(trailing[:, None, :, None], product, 0.0)
    return factored.reshape(parent.shape), panel_rows.reshape(parent_blocks // N_ROW, N_ROW, BS, PW)
```

```python
import itertools
import jax
import jax.numpy as jnp
from jax import lax
from jax.experimental import pallas as pl
from jax.experimental.pallas import tpu as pltpu
from jax.sharding import Mesh, PartitionSpec as P

BS = 256
AXES = ("ylo", "x", "core", "yhi", "z")
SIZES = (2, 4, 2, 2, 4)
NT = (((1,), (1,)), ((), ()))
STEPS = 7


def route(move, keep=lambda dev: True):
    pairs = []
    for spot in itertools.product(*[range(n) for n in SIZES]):
        dev = dict(zip(AXES, spot))
        if not keep(dev):
            continue
        far = dict(dev)
        far.update(move(dev))
        flat = []
        for d in (dev, far):
            i = 0
            for a, n in zip(AXES, SIZES):
                i = i * n + d[a] % n
            flat.append(i)
        pairs.append(tuple(flat))
    return pairs


def send(value, pairs):
    return lax.ppermute(value, AXES, pairs)


def home(dev):
    return 2 * dev["yhi"] + dev["z"] // 2


def away(dev):
    apart = dev["x"] - home(dev)
    return (apart if dev["core"] == 0 else -apart) % 4


def halves(value):
    high = value.astype(jnp.bfloat16)
    return high, (value - high.astype(jnp.float32)).astype(jnp.bfloat16)


def mul3(ah, al, bh, bl):
    def dot(u, v):
        return lax.dot_general(u, v, NT, preferred_element_type=jnp.float32)

    return dot(ah, bh) + (dot(ah, bl) + dot(al, bh))


def place_kernel(where, own, maps, out):
    half = where[0]
    for s in range(4):
        spots = lax.broadcasted_iota(jnp.int32, (BS, BS), 0)
        pick = jnp.where(spots == maps[s, :][None, :], 1.0, 0.0).astype(jnp.bfloat16)
        value = own[s]
        total = None
        for _ in range(3):
            part = value.astype(jnp.bfloat16)
            value = value - part.astype(jnp.float32)
            moved = jnp.dot(pick, part, preferred_element_type=jnp.float32)
            total = moved if total is None else total + moved
        out[lax.rem(half + s, 2), s // 2] = total


def place(half, own, maps):
    return pl.pallas_call(
        place_kernel,
        out_shape=jax.ShapeDtypeStruct((2, 2, BS, 128), jnp.float32),
        in_specs=[
            pl.BlockSpec(memory_space=pltpu.SMEM),
            pl.BlockSpec(memory_space=pltpu.VMEM),
            pl.BlockSpec(memory_space=pltpu.VMEM),
        ],
        out_specs=pl.BlockSpec(memory_space=pltpu.VMEM),
        name="place",
    )(half, own, maps)


def final_kernel(
    spot, child_mask, panel_mask, inv, lead_all, parent, *refs
):
    pieces = refs[:12]
    columns = [refs[12 + STEPS * n : 12 + STEPS * (n + 1)] for n in range(4)]
    (out, panel) = refs[12 + 4 * STEPS : 14 + 4 * STEPS]
    (
        rh, rl, ch, cl, eh, el, lead_o, lead_c, ph, pll, qh, ql, vh, vl, stage_r, stage_c, acc, sems,
    ) = refs[14 + 4 * STEPS :]
    p, x, core, yhi, z = (spot[n] for n in range(5))
    q = 2 * x + core
    c = 4 * yhi + z
    apart = lax.rem(x - (2 * yhi + z // 2) + 4, 4)
    apart = jnp.where(core == 0, apart, lax.rem(4 - apart, 4))
    apart_other = lax.rem(4 - apart, 4)
    slot = pl.program_id(0)

    def put_rows(block, count, high, low, base, z_from, yhi_at):
        for yr in range(2):
            start = pl.multiple_of(z_from * 256 + lax.rem(yhi_at + yr, 2) * 128, 128)
            for i in range(2):
                a, b = halves(block[yr * 2 + i])
                high[base + count * i, :, pl.ds(start, 128)] = a
                low[base + count * i, :, pl.ds(start, 128)] = b

    def put_lead(block, first, lead, base, lane, z_from):
        right = jnp.logical_or(z_from == 1, z_from == 2).astype(jnp.int32)
        at = base + jnp.where(z_from >= 2, 2, 0) + lane
        for half in range(2):
            start = pl.multiple_of(right * 256 + half * 128, 128)
            lead[at, :, pl.ds(start, 128)] = block[first + half]

    @pl.when(slot == 0)
    def _():
        jobs = []
        turn = jnp.where(core == 0, 1, 3)
        turn_c = jnp.where(lax.rem(z, 2) == 0, 1, 3)
        for k in range(4):
            z_from = lax.rem(z + 4 * 4 - turn * k, 4)
            for lane in range(2):
                jobs.append(("row", pieces[3 * k + lane], lane, z_from))
            jobs.append(("lead", pieces[3 * k + 2], 0, z_from))
        for u in range(4):
            z_from = lax.rem(z + 4 * 4 - turn_c * u, 4)
            for n in range(4):
                jobs.append(("col", columns[n], (n, u), z_from))

        def at_of(job, slot_n):
            kind, ref, info, _ = job
            if kind == "row" or kind == "lead":
                return [(None, ref, stage_r.at[slot_n])]
            n, u = info
            dist = apart if n < 2 else apart_other
            return [(u + dist == t, ref[t], stage_c.at[slot_n]) for t in range(u, u + 4)]

        def begin(n):
            for cond, src, dst in at_of(jobs[n], n % 4):
                def go(src=src, dst=dst):
                    pltpu.make_async_copy(src, dst, sems.at[n % 4]).start()
                if cond is None:
                    go()
                else:
                    pl.when(cond)(go)

        def finish(n):
            _, src, dst = at_of(jobs[n], n % 4)[0]
            pltpu.make_async_copy(src, dst, sems.at[n % 4]).wait()

        def use(n):
            kind, _, info, z_from = jobs[n]
            if kind == "row":
                child = lax.rem(p + info, 2)
                put_rows(stage_r.at[n % 4], 1, rh, rl, child * 2, z_from, yhi)
            elif kind == "lead":
                for lane in range(2):
                    put_lead(stage_r.at[n % 4], 2 * lane, lead_o, 0, lane, z_from)
            else:
                which, _ = info
                lane = core if which < 2 else 1 - core
                plane = p if which % 2 == 0 else 1 - p
                child = lax.rem(plane + lane, 2)
                put_rows(stage_c.at[n % 4], 2, ch, cl, child * 4 + plane, z_from, yhi)
                put_lead(stage_c.at[n % 4], 4, lead_c, plane * 4, lane, z_from)

        for n in range(3):
            begin(n)
        a, b = halves(inv[...])
        vh[...] = a
        vl[...] = b
        for j in range(2):
            for k in range(8):
                a, b = halves(lead_all[j, k])
                at = (k % 4) * 256 + (k // 4) * 128
                eh[j, :, at : at + 128] = a
                el[j, :, at : at + 128] = b
        for n in range(len(jobs)):
            if n + 3 < len(jobs):
                begin(n + 3)
            finish(n)
            use(n)

        def panel_of(lead, at):
            ah, al = halves(lead[at])
            left = mul3(ah[:, :256], al[:, :256], vh[:256, :256], vl[:256, :256])
            right = mul3(ah, al, vh[256:, :], vl[256:, :])
            return jnp.concatenate([left, right], axis=1)

        for i in range(2):
            for j in range(2):
                @pl.when(child_mask[0, (p + 2 * i) * 8 + q, j] == 1)
                def _():
                    lead_o[i, :, j * 256 : j * 256 + 256] -= mul3(rh[i], rl[i], eh[j], el[j])

        for i in range(4):
            value = panel_of(lead_o, i)
            panel[i] = value
            a, b = halves(value)
            ph[i] = a
            pll[i] = b

        for plane in range(2):
            for i in range(2):
                for j in range(2):
                    @pl.when(child_mask[0, (plane + 2 * i) * 8 + c, j] == 1)
                    def _():
                        s = plane + 2 * i
                        lead_c[plane * 4 + i, :, j * 256 : j * 256 + 256] -= mul3(
                            ch[s], cl[s], eh[j], el[j]
                        )

        for n in range(8):
            a, b = halves(panel_of(lead_c, n))
            qh[n] = a
            ql[n] = b

    row_block = 16 * slot + 8 * p + q
    for j in range(8):
        for half in range(2):
            acc[:, half * 128 : half * 128 + 128] = parent[pl.ds(2 * j + half, BS, stride=16), :]
        for child in range(2):
            s = j - 2 * child
            if s < 0 or s >= 4:
                continue
            i = jnp.clip(slot - child, 0, 1)
            listed = child_mask[child, (p + 2 * i) * 8 + q, s * 8 + c] == 1
            @pl.when(jnp.logical_and(listed, slot - child == i))
            def _():
                acc[...] -= mul3(rh[child * 2 + i], rl[child * 2 + i], ch[child * 4 + s], cl[child * 4 + s])
        col_block = 8 * j + c
        trailing = jnp.logical_and(row_block >= 2, col_block >= 2)
        @pl.when(jnp.logical_and(trailing, panel_mask[row_block, col_block] == 1))
        def _():
            n = (j % 2) * 4 + j // 2
            acc[...] -= mul3(ph[slot], pll[slot], qh[n], ql[n])
        for half in range(2):
            out[pl.ds(2 * j + half, BS, stride=16), :] = acc[:, half * 128 : half * 128 + 128]


def finish_all(spot, child_mask, panel_mask, inv, lead_all, parent, pieces, columns):
    f32, bf16 = jnp.float32, jnp.bfloat16
    vmem = pl.BlockSpec(memory_space=pltpu.VMEM)
    smem = pl.BlockSpec(memory_space=pltpu.SMEM)
    far = pl.BlockSpec(memory_space=pl.ANY)
    arrays = list(pieces) + [ref for group in columns for ref in group]
    return pl.pallas_call(
        final_kernel,
        grid=(4,),
        out_shape=(
            jax.ShapeDtypeStruct((4 * BS * 16, 128), f32),
            jax.ShapeDtypeStruct((4, BS, 512), f32),
        ),
        in_specs=[smem, smem, smem, vmem, vmem, pl.BlockSpec((BS * 16, 128), lambda i: (i, 0))]
        + [far] * len(arrays),
        out_specs=(
            pl.BlockSpec((BS * 16, 128), lambda i: (i, 0)),
            pl.BlockSpec((4, BS, 512), lambda i: (0, 0, 0)),
        ),
        scratch_shapes=[
            pltpu.VMEM((4, BS, 1024), bf16),
            pltpu.VMEM((4, BS, 1024), bf16),
            pltpu.VMEM((8, BS, 1024), bf16),
            pltpu.VMEM((8, BS, 1024), bf16),
            pltpu.VMEM((2, BS, 1024), bf16),
            pltpu.VMEM((2, BS, 1024), bf16),
            pltpu.VMEM((4, BS, 512), f32),
            pltpu.VMEM((8, BS, 512), f32),
            pltpu.VMEM((4, BS, 512), bf16),
            pltpu.VMEM((4, BS, 512), bf16),
            pltpu.VMEM((8, BS, 512), bf16),
            pltpu.VMEM((8, BS, 512), bf16),
            pltpu.VMEM((512, 512), bf16),
            pltpu.VMEM((512, 512), bf16),
            pltpu.VMEM((4, 4, BS, 128), f32),
            pltpu.VMEM((4, 6, BS, 128), f32),
            pltpu.VMEM((BS, BS), f32),
            pltpu.SemaphoreType.DMA((4,)),
        ],
        compiler_params=pltpu.CompilerParams(vmem_limit_bytes=52 * 1024 * 1024),
        cost_estimate=pl.CostEstimate(flops=22_000_000_000, bytes_accessed=36_000_000, transcendentals=0),
        name="finish",
    )(spot, child_mask, panel_mask, inv, lead_all, parent, *arrays)


def shards(child_factor, parent, row_map, child_listed, inv_diag, panel_listed):
    p, x, core, yhi, z = (lax.axis_index(a) for a in AXES)
    spot = jnp.stack([p, x, core, yhi, z]).astype(jnp.int32)
    q = 2 * x + core
    first = core == 0
    own = child_factor.reshape(4, BS, 128)
    own_map = lax.dynamic_slice(row_map.reshape(2, 4, 8, BS), (p, 0, q, 0), (1, 4, 1, BS)).reshape(4, BS)
    placed = place(spot[:1], own, own_map)
    mine, other = placed[0], placed[1]

    flat = parent.reshape(4 * BS * 16, 128)
    lead = parent.reshape(4, BS, 16, 128)[:, :, :2, :].transpose(0, 2, 1, 3)

    source = jnp.where((p == 0) & (x == 0), mine[0], 0.0)
    lead_all = lax.all_gather(lax.psum(source, ("ylo", "x")), ("core", "yhi", "z")).reshape(2, 8, BS, 128)

    near = send(mine, route(lambda d: {"yhi": 1 - d["yhi"]}))
    cross = send(other, route(lambda d: {"ylo": 1 - d["ylo"]}))
    cross_far = send(other, route(lambda d: {"ylo": 1 - d["ylo"], "yhi": 1 - d["yhi"]}))
    spread = send(lead[2:], route(lambda d: {"z": 3 - d["z"]}, lambda d: d["yhi"] == 0 and d["z"] < 2))
    lead_piece = jnp.where(z < 2, lead[:2], spread)
    spread = send(lead_piece, route(lambda d: {"yhi": 1}, lambda d: d["yhi"] == 0))
    lead_piece = jnp.where(yhi == 0, lead_piece, spread).reshape(4, BS, 128)

    blocks = [
        jnp.stack([mine, near]).reshape(4, BS, 128),
        jnp.stack([cross, cross_far]).reshape(4, BS, 128),
        lead_piece,
    ]
    ring = route(lambda d: {"z": d["z"] + (1 if d["core"] == 0 else -1)})
    rounds = [blocks]
    for _ in range(3):
        rounds.append([send(block, ring) for block in rounds[-1]])

    to_twin = route(
        lambda d: {"core": 1 - d["core"]}, lambda d: d["x"] == home(d) and d["core"] == d["z"] % 2
    )
    holder = core == z % 2
    units = []
    for own_child, cross_child, leads in rounds:
        kept = jnp.concatenate(
            [jnp.where(first, own_child, cross_child), jnp.where(first, leads[:2], leads[2:])]
        )
        given = jnp.concatenate(
            [jnp.where(first, cross_child, own_child), jnp.where(first, leads[2:], leads[:2])]
        )
        units.append(jnp.where(holder, kept, send(given, to_twin)))

    apart = (x - (2 * yhi + z // 2)) % 4
    apart = jnp.where(first, apart, (-apart) % 4)
    chain = []
    received = None
    for t in range(STEPS):
        if t == 0:
            now = units[0]
        elif t < 4:
            now = jnp.where(apart == 0, units[t], received)
        else:
            now = received
        chain.append(now)
        if t < STEPS - 1:
            received = send(
                now,
                route(
                    lambda d: {"x": d["x"] + (1 if d["core"] == 0 else -1)},
                    lambda d: away(d) < 3 and 0 <= t - away(d) <= 3,
                ),
            )
    swapped, twin, twin_swapped = [], [], []
    for t in range(STEPS):
        good = lambda d: 0 <= t - away(d) <= 3
        swapped.append(send(chain[t], route(lambda d: {"ylo": 1 - d["ylo"]}, good)))
        twin.append(send(chain[t], route(lambda d: {"core": 1 - d["core"]}, good)))
        twin_swapped.append(send(swapped[t], route(lambda d: {"core": 1 - d["core"]}, good)))

    factored, panel = finish_all(
        spot,
        child_listed,
        panel_listed,
        inv_diag,
        lead_all,
        flat,
        [piece for group in rounds for piece in group],
        [chain, swapped, twin, twin_swapped],
    )
    return factored.reshape(parent.shape), panel.reshape(4, 1, BS, 512)


def solution(mesh):
    grid = Mesh(mesh.devices.reshape(SIZES), AXES)
    row, col = ("ylo", "x", "core"), ("yhi", "z")
    return jax.shard_map(
        shards,
        mesh=grid,
        in_specs=(
            P(None, row, None, col),
            P(None, row, None, None, col, None),
            P(),
            P(),
            P(),
            P(),
        ),
        out_specs=(P(None, row, None, None, col, None), P(None, row, None, None)),
        check_vma=False,
    )
```

```python
import functools
import itertools
import jax
import jax.numpy as jnp
from jax import lax
from jax.experimental import pallas as pl
from jax.experimental.pallas import tpu as pltpu
from jax.sharding import Mesh, PartitionSpec as P

BS = 256
AXES = ("ylo", "x", "core", "yhi", "z")
SIZES = (2, 4, 2, 2, 4)
NT = (((1,), (1,)), ((), ()))


def route(move, keep=lambda dev: True):
    pairs = []
    for spot in itertools.product(*[range(n) for n in SIZES]):
        dev = dict(zip(AXES, spot))
        if not keep(dev):
            continue
        far = dict(dev)
        far.update(move(dev))
        flat = []
        for d in (dev, far):
            i = 0
            for a, n in zip(AXES, SIZES):
                i = i * n + d[a] % n
            flat.append(i)
        pairs.append(tuple(flat))
    return pairs


def send(value, pairs):
    return lax.ppermute(value, AXES, pairs)


def home(dev):
    return 2 * dev["yhi"] + dev["z"] // 2


def away(dev):
    apart = dev["x"] - home(dev)
    return (apart if dev["core"] == 0 else -apart) % 4


def halves(value):
    high = value.astype(jnp.bfloat16)
    return high, (value - high.astype(jnp.float32)).astype(jnp.bfloat16)


def mul3(ah, al, bh, bl):
    def dot(u, v):
        return lax.dot_general(u, v, NT, preferred_element_type=jnp.float32)

    return dot(ah, bh) + (dot(ah, bl) + dot(al, bh))


def place_kernel(where, own, maps, out, token):
    half = where[0]
    token[...] = jnp.zeros_like(token)
    for s in range(4):
        spots = lax.broadcasted_iota(jnp.int32, (BS, BS), 0)
        pick = jnp.where(spots == maps[s, :][None, :], 1.0, 0.0).astype(jnp.bfloat16)
        value = own[s]
        total = None
        for _ in range(3):
            part = value.astype(jnp.bfloat16)
            value = value - part.astype(jnp.float32)
            moved = jnp.dot(pick, part, preferred_element_type=jnp.float32)
            total = moved if total is None else total + moved
        out[lax.rem(half + s, 2), s // 2] = total


def place(half, own, maps):
    return pl.pallas_call(
        place_kernel,
        out_shape=(
            jax.ShapeDtypeStruct((2, 2, BS, 128), jnp.float32),
            jax.ShapeDtypeStruct((8, 128), jnp.float32),
        ),
        in_specs=[
            pl.BlockSpec(memory_space=pltpu.SMEM),
            pl.BlockSpec(memory_space=pltpu.VMEM),
            pl.BlockSpec(memory_space=pltpu.VMEM),
        ],
        out_specs=[pl.BlockSpec(memory_space=pltpu.VMEM)] * 2,
        name="place",
    )(half, own, maps)


def rows_kernel(spot, child_mask, inv, *refs):
    gathered = refs[0:4]
    leads = refs[4:8]
    edge_twin = refs[8]
    panel, to_send, rh, rl, ph, pll = refs[9:15]
    eh, el, lead, vh, vl = refs[15:]
    p, x, core, yhi, z = (spot[n] for n in range(5))
    q = 2 * x + core
    turn = jnp.where(core == 0, 1, 3)

    a, b = halves(inv[...])
    vh[...] = a
    vl[...] = b
    for k in range(4):
        own_z = lax.rem(z + 16 - turn * k, 4)
        twin_z = lax.rem(z + turn * k, 4)
        for yr in range(2):
            y_at = lax.rem(yhi + yr, 2)
            start = pl.multiple_of(own_z * 256 + y_at * 128, 128)
            for lane in range(2):
                child = lax.rem(p + lane, 2)
                for i in range(2):
                    a, b = halves(gathered[k][lane * 4 + yr * 2 + i])
                    rh[child * 2 + i, :, pl.ds(start, 128)] = a
                    rl[child * 2 + i, :, pl.ds(start, 128)] = b
            a, b = halves(leads[k][4 + yr])
            eh[core, :, pl.ds(start, 128)] = a
            el[core, :, pl.ds(start, 128)] = b
            start = pl.multiple_of(twin_z * 256 + y_at * 128, 128)
            a, b = halves(edge_twin[k * 2 + yr])
            eh[1 - core, :, pl.ds(start, 128)] = a
            el[1 - core, :, pl.ds(start, 128)] = b
        right = jnp.logical_or(own_z == 1, own_z == 2).astype(jnp.int32)
        for lane in range(2):
            at = jnp.where(own_z >= 2, 2, 0) + lane
            for half in range(2):
                start = pl.multiple_of(right * 256 + half * 128, 128)
                lead[at, :, pl.ds(start, 128)] = leads[k][lane * 2 + half]

    for j in range(2):
        change = mul3(
            rh[0:2].reshape(512, 1024), rl[0:2].reshape(512, 1024), eh[j], el[j]
        )
        for i in range(2):
            listed = child_mask[0, (p + 2 * i) * 8 + q, j] == 1
            part = change[i * 256 : i * 256 + 256]
            lead[i, :, j * 256 : j * 256 + 256] -= jnp.where(listed, part, 0.0)

    for pair in range(2):
        ah, al = halves(lead[2 * pair : 2 * pair + 2].reshape(512, 512))
        left = mul3(ah[:, :256], al[:, :256], vh[:256, :256], vl[:256, :256])
        right = mul3(ah, al, vh[256:, :], vl[256:, :])
        for half, value in enumerate((left, right)):
            a, b = halves(value)
            cols = slice(half * 256, half * 256 + 256)
            for i in range(2):
                rows = slice(i * 256, i * 256 + 256)
                panel[2 * pair + i, :, cols] = value[rows]
                ph[2 * pair + i, :, cols] = a[rows]
                pll[2 * pair + i, :, cols] = b[rows]
                for n in range(2):
                    to_send[2 * pair + i, 2 * half + n] = value[rows, n * 128 : n * 128 + 128]


def rows_step(spot, child_mask, inv, gathered, leads, edge_twin):
    f32, bf16 = jnp.float32, jnp.bfloat16
    vmem = pl.BlockSpec(memory_space=pltpu.VMEM)
    smem = pl.BlockSpec(memory_space=pltpu.SMEM)
    return pl.pallas_call(
        rows_kernel,
        out_shape=(
            jax.ShapeDtypeStruct((4, BS, 512), f32),
            jax.ShapeDtypeStruct((4, 4, BS, 128), f32),
            jax.ShapeDtypeStruct((4, BS, 1024), bf16),
            jax.ShapeDtypeStruct((4, BS, 1024), bf16),
            jax.ShapeDtypeStruct((4, BS, 512), bf16),
            jax.ShapeDtypeStruct((4, BS, 512), bf16),
        ),
        in_specs=[smem, smem] + [vmem] * 10,
        out_specs=[vmem] * 6,
        scratch_shapes=[
            pltpu.VMEM((2, BS, 1024), bf16),
            pltpu.VMEM((2, BS, 1024), bf16),
            pltpu.VMEM((4, BS, 512), f32),
            pltpu.VMEM((512, 512), bf16),
            pltpu.VMEM((512, 512), bf16),
        ],
        compiler_params=pltpu.CompilerParams(vmem_limit_bytes=40 * 1024 * 1024),
        cost_estimate=pl.CostEstimate(flops=4_000_000_000, bytes_accessed=18_000_000, transcendentals=0),
        name="rows",
    )(spot, child_mask, inv, *gathered, *leads, edge_twin)


def update_kernel(spot, child_mask, parent, rh, rl, *refs):
    arrays, (out, ch, cl, acc) = refs[:8], refs[8:]
    p, x, core, yhi, z = (spot[n] for n in range(5))
    q = 2 * x + core
    c = 4 * yhi + z
    slot = pl.program_id(0)

    @pl.when(slot == 0)
    def _():
        for n in range(8):
            lane = core if n < 4 else 1 - core
            z_from = lax.rem(z + x + (0, 1, 3, 2)[n % 4] - (2 * yhi + z // 2) + 4, 4)
            for part in range(2):
                plane = p if part == 0 else 1 - p
                child = lax.rem(plane + lane, 2)
                for yr in range(2):
                    start = pl.multiple_of(z_from * 256 + lax.rem(yhi + yr, 2) * 128, 128)
                    for i in range(2):
                        a, b = halves(arrays[n][part * 4 + yr * 2 + i])
                        ch[child * 4 + plane + 2 * i, :, pl.ds(start, 128)] = a
                        cl[child * 4 + plane + 2 * i, :, pl.ds(start, 128)] = b

    for j in range(8):
        touched = j < 6
        for half in range(2):
            at = pl.ds(2 * j + half, BS, stride=16)
            if touched:
                acc[:, half * 128 : half * 128 + 128] = parent[at, :]
            else:
                out[at, :] = parent[at, :]
        if not touched:
            continue
        for child in range(2):
            s = j - 2 * child
            if s < 0 or s >= 4:
                continue
            i = jnp.clip(slot - child, 0, 1)
            listed = child_mask[child, (p + 2 * i) * 8 + q, s * 8 + c] == 1

            @pl.when(jnp.logical_and(listed, slot - child == i))
            def _():
                acc[...] -= mul3(
                    rh[child * 2 + i], rl[child * 2 + i], ch[child * 4 + s], cl[child * 4 + s]
                )

        for half in range(2):
            out[pl.ds(2 * j + half, BS, stride=16), :] = acc[:, half * 128 : half * 128 + 128]


def update_step(spot, child_mask, flat, rh, rl, arrays):
    vmem = pl.BlockSpec(memory_space=pltpu.VMEM)
    smem = pl.BlockSpec(memory_space=pltpu.SMEM)
    block = pl.BlockSpec((BS * 16, 128), lambda i: (i, 0))
    return pl.pallas_call(
        update_kernel,
        grid=(4,),
        out_shape=jax.ShapeDtypeStruct(flat.shape, jnp.float32),
        in_specs=[smem, smem, block] + [vmem] * (2 + len(arrays)),
        out_specs=block,
        scratch_shapes=[
            pltpu.VMEM((8, BS, 1024), jnp.bfloat16),
            pltpu.VMEM((8, BS, 1024), jnp.bfloat16),
            pltpu.VMEM((BS, BS), jnp.float32),
        ],
        compiler_params=pltpu.CompilerParams(vmem_limit_bytes=40 * 1024 * 1024),
        cost_estimate=pl.CostEstimate(flops=6_400_000_000, bytes_accessed=28_000_000, transcendentals=0),
        name="update",
    )(spot, child_mask, flat, rh, rl, *arrays)


def trail_kernel(spot, panel_mask, assembled, ph, pll, *refs):
    arrays, (out, qh, ql) = refs[:8], refs[8:]
    p, x, core, yhi, z = (spot[n] for n in range(5))
    r = 8 * p + 2 * x + core
    c = 4 * yhi + z
    right, slot = pl.program_id(0), pl.program_id(1)

    @pl.when(jnp.logical_and(right == 0, slot == 0))
    def _():
        for n in range(8):
            lane = core if n < 4 else 1 - core
            from_slot = lax.rem(x + (0, 1, 3, 2)[n % 4] - (2 * yhi + z // 2) + 4, 4)
            for part in range(2):
                plane = p if part == 0 else 1 - p
                for half in range(2):
                    start = pl.multiple_of(lane * 256 + half * 128, 128)
                    a, b = halves(arrays[n][part * 2 + half])
                    qh[plane * 4 + from_slot, :, pl.ds(start, 128)] = a
                    ql[plane * 4 + from_slot, :, pl.ds(start, 128)] = b

    row_block = 16 * slot + r
    for jj in range(4):
        j = 4 * right + jj
        col_block = 8 * j + c
        n = lax.rem(j, 2) * 4 + j // 2
        use = jnp.logical_and(row_block >= 2, col_block >= 2)
        use = jnp.logical_and(use, panel_mask[row_block, col_block] == 1)

        @pl.when(use)
        def _():
            product = mul3(ph[slot], pll[slot], qh[n], ql[n])
            for half in range(2):
                out[:, 2 * jj + half, :] = (
                    assembled[:, 2 * jj + half, :] - product[:, half * 128 : half * 128 + 128]
                )

        @pl.when(jnp.logical_not(use))
        def _():
            for half in range(2):
                out[:, 2 * jj + half, :] = assembled[:, 2 * jj + half, :]


def trail_step(spot, panel_mask, assembled, ph, pll, arrays):
    vmem = pl.BlockSpec(memory_space=pltpu.VMEM)
    smem = pl.BlockSpec(memory_space=pltpu.SMEM)
    block = pl.BlockSpec((BS, 8, 128), lambda j, i: (i, j, 0))
    return pl.pallas_call(
        trail_kernel,
        grid=(2, 4),
        out_shape=jax.ShapeDtypeStruct((4 * BS, 16, 128), jnp.float32),
        in_specs=[smem, smem, block] + [vmem] * (2 + len(arrays)),
        out_specs=block,
        scratch_shapes=[
            pltpu.VMEM((8, BS, 512), jnp.bfloat16),
            pltpu.VMEM((8, BS, 512), jnp.bfloat16),
        ],
        compiler_params=pltpu.CompilerParams(vmem_limit_bytes=40 * 1024 * 1024),
        cost_estimate=pl.CostEstimate(flops=6_400_000_000, bytes_accessed=22_000_000, transcendentals=0),
        name="trail",
    )(spot, panel_mask, assembled, ph, pll, *arrays)


def gate_kernel(*refs):
    pass


def gate(values, after):
    far = pl.BlockSpec(memory_space=pl.ANY)
    return pl.pallas_call(
        gate_kernel,
        out_shape=[jax.ShapeDtypeStruct(v.shape, v.dtype) for v in values],
        in_specs=[far] * (len(values) + len(after)),
        out_specs=[far] * len(values),
        input_output_aliases={i: i for i in range(len(values))},
        compiler_params=pltpu.CompilerParams(vmem_limit_bytes=1024 * 1024),
        cost_estimate=pl.CostEstimate(flops=0, bytes_accessed=0, transcendentals=0),
        name="gate",
    )(*values, *after)


def shards(child_factor, parent, row_map, child_listed, inv_diag, panel_listed):
    p, x, core, yhi, z = (lax.axis_index(a) for a in AXES)
    spot = jnp.stack([p, x, core, yhi, z]).astype(jnp.int32)
    q = 2 * x + core
    first = core == 0
    own = child_factor.reshape(4, BS, 128)
    own_map = lax.dynamic_slice(row_map.reshape(2, 4, 8, BS), (p, 0, q, 0), (1, 4, 1, BS)).reshape(4, BS)
    placed, nothing = place(spot[:1], own, own_map)
    mine, other = placed[0], placed[1]

    late = parent.reshape(4, BS, 16, 128)[:, :, :2, :].transpose(0, 2, 1, 3) + nothing[0, 0]
    flat = parent.reshape(4 * BS * 16, 128)
    edge = mine[0]

    at_zero = lambda d: d["ylo"] == 0 and d["x"] == 0
    near = send(mine, route(lambda d: {"yhi": 1 - d["yhi"]}))
    cross = send(other, route(lambda d: {"ylo": 1 - d["ylo"]}))
    cross_far = send(other, route(lambda d: {"ylo": 1 - d["ylo"], "yhi": 1 - d["yhi"]}))
    spread = send(late[2:], route(lambda d: {"z": 3 - d["z"]}, lambda d: d["yhi"] == 0 and d["z"] < 2))
    moved = [send(edge, route(lambda d: {"x": n}, at_zero)) for n in (1, 3, 2)]
    near, cross, cross_far, spread, *moved = gate([near, cross, cross_far, spread] + moved, [])

    block = jnp.concatenate([mine, near, cross, cross_far])
    lead_piece = jnp.where(z < 2, late[:2], spread)
    edge = jnp.where(x == 0, edge, jnp.where(x == 1, moved[0], jnp.where(x == 3, moved[1], moved[2])))

    ring = route(lambda d: {"z": d["z"] + (1 if d["core"] == 0 else -1)})
    twin = route(lambda d: {"core": 1 - d["core"]})
    swap = route(lambda d: {"ylo": 1 - d["ylo"]})
    around = [route(lambda d: {"x": d["x"] - n}) for n in (1, 3, 2)]

    def target(lane):
        def move(d):
            z_to = 2 * (d["x"] % 2) + d["core"]
            return {"x": d["x"] + d["z"] - z_to, "z": z_to, "core": lane}

        return route(move, lambda d: d["yhi"] == d["x"] // 2)

    def scatter(parts):
        return [send(part, target(lane)) for lane, part in enumerate(parts)]

    gathered = [block]
    low = lambda d: d["ylo"] == 0
    arrived = send(block, ring)
    spread = send(lead_piece, route(lambda d: {"yhi": 1}, lambda d: d["yhi"] == 0))
    edge_up = send(edge, route(lambda d: {"ylo": 1}, low))
    edge_far = send(edge, route(lambda d: {"yhi": 1 - d["yhi"]}, low))
    edge_up_far = send(edge, route(lambda d: {"ylo": 1, "yhi": 1 - d["yhi"]}, low))
    pieces = scatter([block[:4], block[4:]])
    arrived, spread, edge_up, edge_far, edge_up_far, *pieces = gate(
        [arrived, spread, edge_up, edge_far, edge_up_far] + pieces, []
    )
    gathered.append(arrived)
    lead_piece = jnp.where(yhi == 0, lead_piece, spread).reshape(4, BS, 128)
    edge = jnp.stack([jnp.where(p == 0, edge, edge_up), jnp.where(p == 0, edge_far, edge_up_far)])
    leads = [jnp.concatenate([lead_piece, edge])]
    quarter = jnp.where(first, pieces[0], pieces[1])

    arrived = send(gathered[-1], ring)
    lead_next = send(leads[-1], ring)
    other_quarter = send(quarter, swap)
    arrived, lead_next, other_quarter = gate([arrived, lead_next, other_quarter], [])
    gathered.append(arrived)
    leads.append(lead_next)

    columns = [jnp.concatenate([quarter, other_quarter])]
    arrived = send(gathered[-1], ring)
    lead_next = send(leads[-1], ring)
    moving = [send(columns[0], pairs) for pairs in around]
    arrived, lead_next = gate([arrived, lead_next], [])
    gathered.append(arrived)
    leads.append(lead_next)
    leads.append(send(leads[-1], ring))
    moving = gate(moving + [leads[-1]], [])
    columns += moving[:3]
    leads[-1] = moving[3]

    edge_own = jnp.concatenate([block[4:] for block in leads])
    edge_twin = send(edge_own, twin)
    panel, to_send, rh, rl, ph, pll = rows_step(
        spot, child_listed, inv_diag, gathered, leads, edge_twin
    )
    turn = (z - (2 * (x % 2) + core)) % 4
    mine = lax.dynamic_index_in_dim(to_send, turn, 0, keepdims=False)
    pieces = scatter([mine[:2], mine[2:]])
    arrays = [send(value, twin) for value in columns[:2]]
    *pieces, arrays[0], arrays[1] = gate(pieces + arrays, [])
    quarter = jnp.where(first, pieces[0], pieces[1])
    other_quarter = send(quarter, swap)
    arrays += [send(value, twin) for value in columns[2:]]
    other_quarter, arrays[2], arrays[3] = gate([other_quarter] + arrays[2:], [])
    panels = [jnp.concatenate([quarter, other_quarter])]
    panels += [send(panels[0], pairs) for pairs in around]
    assembled = update_step(spot, child_listed, flat, rh, rl, columns + arrays)
    panels[1:] = gate(panels[1:], [assembled])
    panels += [send(value, twin) for value in panels]
    factored = trail_step(
        spot, panel_listed, assembled.reshape(4 * BS, 16, 128), ph, pll, panels
    )
    return factored.reshape(parent.shape), panel.reshape(4, 1, BS, 512)


def solution(mesh):
    grid = Mesh(mesh.devices.reshape(SIZES), AXES)
    row, col = ("ylo", "x", "core"), ("yhi", "z")
    return jax.shard_map(
        shards,
        mesh=grid,
        in_specs=(
            P(None, row, None, col),
            P(None, row, None, None, col, None),
            P(),
            P(),
            P(),
            P(),
        ),
        out_specs=(P(None, row, None, None, col, None), P(None, row, None, None)),
        check_vma=False,
    )
```

```python
import functools
import itertools
import jax
import jax.numpy as jnp
from jax import lax
from jax.experimental import pallas as pl
from jax.experimental.pallas import tpu as pltpu
from jax.sharding import Mesh, PartitionSpec as P

BS = 256
AXES = ("ylo", "x", "core", "yhi", "z")
SIZES = (2, 4, 2, 2, 4)
NT = (((1,), (1,)), ((), ()))


def route(move, keep=lambda dev: True):
    pairs = []
    for spot in itertools.product(*[range(n) for n in SIZES]):
        dev = dict(zip(AXES, spot))
        if not keep(dev):
            continue
        far = dict(dev)
        far.update(move(dev))
        flat = []
        for d in (dev, far):
            i = 0
            for a, n in zip(AXES, SIZES):
                i = i * n + d[a] % n
            flat.append(i)
        pairs.append(tuple(flat))
    return pairs


def send(value, pairs):
    return lax.ppermute(value, AXES, pairs)


def home(dev):
    return 2 * dev["yhi"] + dev["z"] // 2


def away(dev):
    apart = dev["x"] - home(dev)
    return (apart if dev["core"] == 0 else -apart) % 4


def halves(value):
    high = value.astype(jnp.bfloat16)
    return high, (value - high.astype(jnp.float32)).astype(jnp.bfloat16)


def mul3(ah, al, bh, bl):
    def dot(u, v):
        return lax.dot_general(u, v, NT, preferred_element_type=jnp.float32)

    return dot(ah, bh) + (dot(ah, bl) + dot(al, bh))


def place_kernel(where, own, maps, out, token):
    half = where[0]
    token[...] = jnp.zeros_like(token)
    for s in range(4):
        spots = lax.broadcasted_iota(jnp.int32, (BS, BS), 0)
        pick = jnp.where(spots == maps[s, :][None, :], 1.0, 0.0).astype(jnp.bfloat16)
        value = own[s]
        total = None
        for _ in range(3):
            part = value.astype(jnp.bfloat16)
            value = value - part.astype(jnp.float32)
            moved = jnp.dot(pick, part, preferred_element_type=jnp.float32)
            total = moved if total is None else total + moved
        out[lax.rem(half + s, 2), s // 2] = total


def place(half, own, maps):
    return pl.pallas_call(
        place_kernel,
        out_shape=(
            jax.ShapeDtypeStruct((2, 2, BS, 128), jnp.float32),
            jax.ShapeDtypeStruct((8, 128), jnp.float32),
        ),
        in_specs=[
            pl.BlockSpec(memory_space=pltpu.SMEM),
            pl.BlockSpec(memory_space=pltpu.VMEM),
            pl.BlockSpec(memory_space=pltpu.VMEM),
        ],
        out_specs=[pl.BlockSpec(memory_space=pltpu.VMEM)] * 2,
        name="place",
    )(half, own, maps)


def rows_kernel(spot, child_mask, inv, *refs):
    sources = refs[0:9]
    panel, to_send, rh, rl, ph, pll = refs[9:15]
    eh, el, lead, vh, vl, held, held_leads, edge_twin, sems = refs[15:]
    gathered = [held.at[k] for k in range(4)]
    leads = [held_leads.at[k] for k in range(4)]
    copies = [
        pltpu.make_async_copy(source, spot_of, sems.at[n])
        for n, (source, spot_of) in enumerate(zip(sources, gathered + leads + [edge_twin]))
    ]
    for n in (0, 4, 8, 1, 5, 2, 6, 3, 7):
        copies[n].start()
    p, x, core, yhi, z = (spot[n] for n in range(5))
    q = 2 * x + core
    turn = jnp.where(core == 0, 1, 3)

    a, b = halves(inv[...])
    vh[...] = a
    vl[...] = b
    copies[8].wait()
    for k in range(4):
        copies[k].wait()
        copies[4 + k].wait()
        own_z = lax.rem(z + 16 - turn * k, 4)
        twin_z = lax.rem(z + turn * k, 4)
        for yr in range(2):
            y_at = lax.rem(yhi + yr, 2)
            start = pl.multiple_of(own_z * 256 + y_at * 128, 128)
            for lane in range(2):
                child = lax.rem(p + lane, 2)
                for i in range(2):
                    a, b = halves(gathered[k][lane * 4 + yr * 2 + i])
                    rh[child * 2 + i, :, pl.ds(start, 128)] = a
                    rl[child * 2 + i, :, pl.ds(start, 128)] = b
            a, b = halves(leads[k][4 + yr])
            eh[core, :, pl.ds(start, 128)] = a
            el[core, :, pl.ds(start, 128)] = b
            start = pl.multiple_of(twin_z * 256 + y_at * 128, 128)
            a, b = halves(edge_twin[k * 2 + yr])
            eh[1 - core, :, pl.ds(start, 128)] = a
            el[1 - core, :, pl.ds(start, 128)] = b
        right = jnp.logical_or(own_z == 1, own_z == 2).astype(jnp.int32)
        for lane in range(2):
            at = jnp.where(own_z >= 2, 2, 0) + lane
            for half in range(2):
                start = pl.multiple_of(right * 256 + half * 128, 128)
                lead[at, :, pl.ds(start, 128)] = leads[k][lane * 2 + half]

    for j in range(2):
        change = mul3(
            rh[0:2].reshape(512, 1024), rl[0:2].reshape(512, 1024), eh[j], el[j]
        )
        for i in range(2):
            listed = child_mask[0, (p + 2 * i) * 8 + q, j] == 1
            part = change[i * 256 : i * 256 + 256]
            lead[i, :, j * 256 : j * 256 + 256] -= jnp.where(listed, part, 0.0)

    for pair in range(2):
        ah, al = halves(lead[2 * pair : 2 * pair + 2].reshape(512, 512))
        left = mul3(ah[:, :256], al[:, :256], vh[:256, :256], vl[:256, :256])
        right = mul3(ah, al, vh[256:, :], vl[256:, :])
        for half, value in enumerate((left, right)):
            a, b = halves(value)
            cols = slice(half * 256, half * 256 + 256)
            for i in range(2):
                rows = slice(i * 256, i * 256 + 256)
                panel[2 * pair + i, :, cols] = value[rows]
                ph[2 * pair + i, :, cols] = a[rows]
                pll[2 * pair + i, :, cols] = b[rows]
                for n in range(2):
                    to_send[2 * pair + i, 2 * half + n] = value[rows, n * 128 : n * 128 + 128]


def rows_step(spot, child_mask, inv, gathered, leads, edge_twin):
    f32, bf16 = jnp.float32, jnp.bfloat16
    vmem = pl.BlockSpec(memory_space=pltpu.VMEM)
    smem = pl.BlockSpec(memory_space=pltpu.SMEM)
    return pl.pallas_call(
        rows_kernel,
        out_shape=(
            jax.ShapeDtypeStruct((4, BS, 512), f32),
            jax.ShapeDtypeStruct((4, 4, BS, 128), f32),
            jax.ShapeDtypeStruct((4, BS, 1024), bf16),
            jax.ShapeDtypeStruct((4, BS, 1024), bf16),
            jax.ShapeDtypeStruct((4, BS, 512), bf16),
            jax.ShapeDtypeStruct((4, BS, 512), bf16),
        ),
        in_specs=[smem, smem, vmem] + [pl.BlockSpec(memory_space=pltpu.HBM)] * 9,
        out_specs=[vmem] * 6,
        scratch_shapes=[
            pltpu.VMEM((2, BS, 1024), bf16),
            pltpu.VMEM((2, BS, 1024), bf16),
            pltpu.VMEM((4, BS, 512), f32),
            pltpu.VMEM((512, 512), bf16),
            pltpu.VMEM((512, 512), bf16),
            pltpu.VMEM((4, 8, BS, 128), f32),
            pltpu.VMEM((4, 6, BS, 128), f32),
            pltpu.VMEM((8, BS, 128), f32),
            pltpu.SemaphoreType.DMA((9,)),
        ],
        compiler_params=pltpu.CompilerParams(vmem_limit_bytes=60 * 1024 * 1024),
        cost_estimate=pl.CostEstimate(flops=4_000_000_000, bytes_accessed=18_000_000, transcendentals=0),
        name="rows",
    )(spot, child_mask, inv, *gathered, *leads, edge_twin)


def update_kernel(spot, child_mask, parent, rh, rl, *refs):
    arrays, (out, ch, cl, acc) = refs[:8], refs[8:]
    p, x, core, yhi, z = (spot[n] for n in range(5))
    q = 2 * x + core
    c = 4 * yhi + z
    slot = pl.program_id(0)

    @pl.when(slot == 0)
    def _():
        for n in range(8):
            lane = core if n < 4 else 1 - core
            z_from = lax.rem(z + x + (0, 1, 3, 2)[n % 4] - (2 * yhi + z // 2) + 4, 4)
            for part in range(2):
                plane = p if part == 0 else 1 - p
                child = lax.rem(plane + lane, 2)
                for yr in range(2):
                    start = pl.multiple_of(z_from * 256 + lax.rem(yhi + yr, 2) * 128, 128)
                    for i in range(2):
                        a, b = halves(arrays[n][part * 4 + yr * 2 + i])
                        ch[child * 4 + plane + 2 * i, :, pl.ds(start, 128)] = a
                        cl[child * 4 + plane + 2 * i, :, pl.ds(start, 128)] = b

    for j in range(8):
        touched = j < 6
        for half in range(2):
            at = pl.ds(2 * j + half, BS, stride=16)
            if touched:
                acc[:, half * 128 : half * 128 + 128] = parent[at, :]
            else:
                out[at, :] = parent[at, :]
        if not touched:
            continue
        for child in range(2):
            s = j - 2 * child
            if s < 0 or s >= 4:
                continue
            i = jnp.clip(slot - child, 0, 1)
            listed = child_mask[child, (p + 2 * i) * 8 + q, s * 8 + c] == 1

            @pl.when(jnp.logical_and(listed, slot - child == i))
            def _():
                acc[...] -= mul3(
                    rh[child * 2 + i], rl[child * 2 + i], ch[child * 4 + s], cl[child * 4 + s]
                )

        for half in range(2):
            out[pl.ds(2 * j + half, BS, stride=16), :] = acc[:, half * 128 : half * 128 + 128]


def update_step(spot, child_mask, flat, rh, rl, arrays):
    vmem = pl.BlockSpec(memory_space=pltpu.VMEM)
    smem = pl.BlockSpec(memory_space=pltpu.SMEM)
    block = pl.BlockSpec((BS * 16, 128), lambda i: (i, 0))
    return pl.pallas_call(
        update_kernel,
        grid=(4,),
        out_shape=jax.ShapeDtypeStruct(flat.shape, jnp.float32),
        in_specs=[smem, smem, block] + [vmem] * (2 + len(arrays)),
        out_specs=block,
        scratch_shapes=[
            pltpu.VMEM((8, BS, 1024), jnp.bfloat16),
            pltpu.VMEM((8, BS, 1024), jnp.bfloat16),
            pltpu.VMEM((BS, BS), jnp.float32),
        ],
        compiler_params=pltpu.CompilerParams(vmem_limit_bytes=40 * 1024 * 1024),
        cost_estimate=pl.CostEstimate(flops=6_400_000_000, bytes_accessed=28_000_000, transcendentals=0),
        name="update",
    )(spot, child_mask, flat, rh, rl, *arrays)


def trail_kernel(spot, panel_mask, assembled, ph, pll, *refs):
    arrays, (out, qh, ql) = refs[:8], refs[8:]
    p, x, core, yhi, z = (spot[n] for n in range(5))
    r = 8 * p + 2 * x + core
    c = 4 * yhi + z
    right, slot = pl.program_id(0), pl.program_id(1)

    @pl.when(jnp.logical_and(right == 0, slot == 0))
    def _():
        for n in range(8):
            lane = core if n < 4 else 1 - core
            from_slot = lax.rem(x + (0, 1, 3, 2)[n % 4] - (2 * yhi + z // 2) + 4, 4)
            for part in range(2):
                plane = p if part == 0 else 1 - p
                for half in range(2):
                    start = pl.multiple_of(lane * 256 + half * 128, 128)
                    a, b = halves(arrays[n][part * 2 + half])
                    qh[plane * 4 + from_slot, :, pl.ds(start, 128)] = a
                    ql[plane * 4 + from_slot, :, pl.ds(start, 128)] = b

    row_block = 16 * slot + r
    for jj in range(4):
        j = 4 * right + jj
        col_block = 8 * j + c
        n = lax.rem(j, 2) * 4 + j // 2
        use = jnp.logical_and(row_block >= 2, col_block >= 2)
        use = jnp.logical_and(use, panel_mask[row_block, col_block] == 1)

        @pl.when(use)
        def _():
            product = mul3(ph[slot], pll[slot], qh[n], ql[n])
            for half in range(2):
                out[:, 2 * jj + half, :] = (
                    assembled[:, 2 * jj + half, :] - product[:, half * 128 : half * 128 + 128]
                )

        @pl.when(jnp.logical_not(use))
        def _():
            for half in range(2):
                out[:, 2 * jj + half, :] = assembled[:, 2 * jj + half, :]


def trail_step(spot, panel_mask, assembled, ph, pll, arrays):
    vmem = pl.BlockSpec(memory_space=pltpu.VMEM)
    smem = pl.BlockSpec(memory_space=pltpu.SMEM)
    block = pl.BlockSpec((BS, 8, 128), lambda j, i: (i, j, 0))
    return pl.pallas_call(
        trail_kernel,
        grid=(2, 4),
        out_shape=jax.ShapeDtypeStruct((4 * BS, 16, 128), jnp.float32),
        in_specs=[smem, smem, block] + [vmem] * (2 + len(arrays)),
        out_specs=block,
        scratch_shapes=[
            pltpu.VMEM((8, BS, 512), jnp.bfloat16),
            pltpu.VMEM((8, BS, 512), jnp.bfloat16),
        ],
        compiler_params=pltpu.CompilerParams(vmem_limit_bytes=40 * 1024 * 1024),
        cost_estimate=pl.CostEstimate(flops=6_400_000_000, bytes_accessed=22_000_000, transcendentals=0),
        name="trail",
    )(spot, panel_mask, assembled, ph, pll, *arrays)


def gate_kernel(*refs):
    pass


def gate(values, after):
    far = pl.BlockSpec(memory_space=pltpu.HBM)
    return pl.pallas_call(
        gate_kernel,
        out_shape=[jax.ShapeDtypeStruct(v.shape, v.dtype) for v in values],
        in_specs=[far] * (len(values) + len(after)),
        out_specs=[far] * len(values),
        input_output_aliases={i: i for i in range(len(values))},
        compiler_params=pltpu.CompilerParams(vmem_limit_bytes=60 * 1024 * 1024),
        cost_estimate=pl.CostEstimate(flops=0, bytes_accessed=0, transcendentals=0),
        name="gate",
    )(*values, *after)


def shards(child_factor, parent, row_map, child_listed, inv_diag, panel_listed):
    p, x, core, yhi, z = (lax.axis_index(a) for a in AXES)
    spot = jnp.stack([p, x, core, yhi, z]).astype(jnp.int32)
    q = 2 * x + core
    first = core == 0
    own = child_factor.reshape(4, BS, 128)
    own_map = lax.dynamic_slice(row_map.reshape(2, 4, 8, BS), (p, 0, q, 0), (1, 4, 1, BS)).reshape(4, BS)
    placed, nothing = place(spot[:1], own, own_map)
    mine, other = placed[0], placed[1]

    late = parent.reshape(4, BS, 16, 128)[:, :, :2, :].transpose(0, 2, 1, 3) + nothing[0, 0]
    flat = parent.reshape(4 * BS * 16, 128)

    edges = lax.all_gather(lax.all_gather(mine[0], "x")[0], ("ylo", "yhi"))[:2]
    edge = jnp.where(yhi == 0, edges, edges[::-1])
    near = send(mine, route(lambda d: {"yhi": 1 - d["yhi"]}))
    cross = send(other, route(lambda d: {"ylo": 1 - d["ylo"]}))
    cross_far = send(other, route(lambda d: {"ylo": 1 - d["ylo"], "yhi": 1 - d["yhi"]}))
    spread = send(late[2:], route(lambda d: {"z": 3 - d["z"]}, lambda d: d["yhi"] == 0 and d["z"] < 2))
    near, cross, cross_far, spread = gate([near, cross, cross_far, spread], [])

    block = jnp.concatenate([mine, near, cross, cross_far])
    lead_piece = jnp.where(z < 2, late[:2], spread)
    ring = route(lambda d: {"z": d["z"] + (1 if d["core"] == 0 else -1)})
    twin = route(lambda d: {"core": 1 - d["core"]})
    swap = route(lambda d: {"ylo": 1 - d["ylo"]})
    around = [route(lambda d: {"x": d["x"] - n}) for n in (1, 3, 2)]

    def target(lane, cross=False):
        def move(d):
            z_to = 2 * (d["x"] % 2) + d["core"]
            plane = d["ylo"] + 1 if cross else d["ylo"]
            return {"ylo": plane, "x": d["x"] + d["z"] - z_to, "z": z_to, "core": lane}

        return route(move, lambda d: d["yhi"] == d["x"] // 2)

    def scatter(parts, cross=False):
        return [send(part, target(lane, cross)) for lane, part in enumerate(parts)]

    gathered = [block]
    arrived = send(block, ring)
    spread = send(lead_piece, route(lambda d: {"yhi": 1}, lambda d: d["yhi"] == 0))
    pieces = scatter([block[:4], block[4:]])
    arrived, spread, *pieces = gate([arrived, spread] + pieces, [])
    gathered.append(arrived)
    lead_piece = jnp.where(yhi == 0, lead_piece, spread).reshape(4, BS, 128)
    leads = [jnp.concatenate([lead_piece, edge])]
    quarter = jnp.where(first, pieces[0], pieces[1])

    arrived = send(gathered[-1], ring)
    lead_next = send(leads[-1], ring)
    other_quarter = send(quarter, swap)
    arrived, lead_next, other_quarter = gate([arrived, lead_next, other_quarter], [])
    gathered.append(arrived)
    leads.append(lead_next)

    columns = [jnp.concatenate([quarter, other_quarter])]
    arrived = send(gathered[-1], ring)
    lead_next = send(leads[-1], ring)
    moving = [send(columns[0], pairs) for pairs in around[:2]]
    arrived, lead_next, *moving = gate([arrived, lead_next] + moving, [])
    gathered.append(arrived)
    leads.append(lead_next)
    columns += moving
    onward = route(lambda d: {"x": d["x"] + (1 if d["core"] == 0 else -1)})
    lead_next = send(leads[-1], ring)
    relayed = send(jnp.where(first, columns[2], columns[1]), onward)
    arrays = [send(value, twin) for value in columns]
    lead_next, relayed, *arrays = gate([lead_next, relayed] + arrays, [])
    leads.append(lead_next)
    columns.append(relayed)

    edge_own = jnp.concatenate([block[4:] for block in leads])
    edge_twin = send(edge_own, twin)
    panel, to_send, rh, rl, ph, pll = rows_step(
        spot, child_listed, inv_diag, gathered, leads, edge_twin
    )
    turn = (z - (2 * (x % 2) + core)) % 4
    mine = lax.dynamic_index_in_dim(to_send, turn, 0, keepdims=False)
    pieces = scatter([mine[:2], mine[2:]]) + scatter([mine[:2], mine[2:]], True)
    arrays.append(send(columns[3], twin))
    assembled = update_step(spot, child_listed, flat, rh, rl, columns + arrays)
    *pieces, assembled = gate(pieces + [assembled], [])
    quarter = jnp.where(first, pieces[0], pieces[1])
    other_quarter = jnp.where(first, pieces[2], pieces[3])
    panels = [jnp.concatenate([quarter, other_quarter])]
    panels += [send(panels[0], pairs) for pairs in around]
    panels += [send(value, twin) for value in panels]
    factored = trail_step(
        spot, panel_listed, assembled.reshape(4 * BS, 16, 128), ph, pll, panels
    )
    return factored.reshape(parent.shape), panel.reshape(4, 1, BS, 512)


def solution(mesh):
    grid = Mesh(mesh.devices.reshape(SIZES), AXES)
    row, col = ("ylo", "x", "core"), ("yhi", "z")
    return jax.shard_map(
        shards,
        mesh=grid,
        in_specs=(
            P(None, row, None, col),
            P(None, row, None, None, col, None),
            P(),
            P(),
            P(),
            P(),
        ),
        out_specs=(P(None, row, None, None, col, None), P(None, row, None, None)),
        check_vma=False,
    )
```

```python
import functools
import itertools
import jax
import jax.numpy as jnp
from jax import lax
from jax.experimental import pallas as pl
from jax.experimental.pallas import tpu as pltpu
from jax.sharding import Mesh, PartitionSpec as P

BS = 256
AXES = ("ylo", "x", "core", "yhi", "z")
SIZES = (2, 4, 2, 2, 4)
NT = (((1,), (1,)), ((), ()))


def route(move, keep=lambda dev: True):
    pairs = []
    for spot in itertools.product(*[range(n) for n in SIZES]):
        dev = dict(zip(AXES, spot))
        if not keep(dev):
            continue
        far = dict(dev)
        far.update(move(dev))
        flat = []
        for d in (dev, far):
            i = 0
            for a, n in zip(AXES, SIZES):
                i = i * n + d[a] % n
            flat.append(i)
        pairs.append(tuple(flat))
    return pairs


def send(value, pairs):
    return lax.ppermute(value, AXES, pairs)


def home(dev):
    return 2 * dev["yhi"] + dev["z"] // 2


def away(dev):
    apart = dev["x"] - home(dev)
    return (apart if dev["core"] == 0 else -apart) % 4


def halves(value):
    high = value.astype(jnp.bfloat16)
    return high, (value - high.astype(jnp.float32)).astype(jnp.bfloat16)


def mul3(ah, al, bh, bl):
    def dot(u, v):
        return lax.dot_general(u, v, NT, preferred_element_type=jnp.float32)

    return dot(ah, bh) + (dot(ah, bl) + dot(al, bh))


def place_kernel(where, own, maps, out, token):
    half = where[0]
    token[...] = jnp.zeros_like(token)
    for s in range(4):
        spots = lax.broadcasted_iota(jnp.int32, (BS, BS), 0)
        pick = jnp.where(spots == maps[s, :][None, :], 1.0, 0.0).astype(jnp.bfloat16)
        value = own[s]
        total = None
        for _ in range(3):
            part = value.astype(jnp.bfloat16)
            value = value - part.astype(jnp.float32)
            moved = jnp.dot(pick, part, preferred_element_type=jnp.float32)
            total = moved if total is None else total + moved
        out[lax.rem(half + s, 2), s // 2] = total


def place(half, own, maps):
    return pl.pallas_call(
        place_kernel,
        out_shape=(
            jax.ShapeDtypeStruct((2, 2, BS, 128), jnp.float32),
            jax.ShapeDtypeStruct((8, 128), jnp.float32),
        ),
        in_specs=[
            pl.BlockSpec(memory_space=pltpu.SMEM),
            pl.BlockSpec(memory_space=pltpu.VMEM),
            pl.BlockSpec(memory_space=pltpu.VMEM),
        ],
        out_specs=[pl.BlockSpec(memory_space=pltpu.VMEM)] * 2,
        name="place",
    )(half, own, maps)


def rows_kernel(spot, child_mask, inv, *refs):
    sources = refs[0:9]
    panel, to_send, rh, rl, ph, pll = refs[9:15]
    eh, el, lead, vh, vl, held, held_leads, edge_twin, sems = refs[15:]
    gathered = [held.at[k] for k in range(4)]
    leads = [held_leads.at[k] for k in range(4)]
    copies = [
        pltpu.make_async_copy(source, spot_of, sems.at[n])
        for n, (source, spot_of) in enumerate(zip(sources, gathered + leads + [edge_twin]))
    ]
    for n in (0, 4, 8, 1, 5, 2, 6, 3, 7):
        copies[n].start()
    p, x, core, yhi, z = (spot[n] for n in range(5))
    q = 2 * x + core
    turn = jnp.where(core == 0, 1, 3)

    a, b = halves(inv[...])
    vh[...] = a
    vl[...] = b
    copies[8].wait()
    for k in range(4):
        copies[k].wait()
        copies[4 + k].wait()
        own_z = lax.rem(z + 16 - turn * k, 4)
        twin_z = lax.rem(z + turn * k, 4)
        for yr in range(2):
            y_at = lax.rem(yhi + yr, 2)
            start = pl.multiple_of(own_z * 256 + y_at * 128, 128)
            for lane in range(2):
                child = lax.rem(p + lane, 2)
                for i in range(2):
                    a, b = halves(gathered[k][lane * 4 + yr * 2 + i])
                    rh[child * 2 + i, :, pl.ds(start, 128)] = a
                    rl[child * 2 + i, :, pl.ds(start, 128)] = b
            a, b = halves(leads[k][4 + yr])
            eh[core, :, pl.ds(start, 128)] = a
            el[core, :, pl.ds(start, 128)] = b
            start = pl.multiple_of(twin_z * 256 + y_at * 128, 128)
            a, b = halves(edge_twin[k * 2 + yr])
            eh[1 - core, :, pl.ds(start, 128)] = a
            el[1 - core, :, pl.ds(start, 128)] = b
        right = jnp.logical_or(own_z == 1, own_z == 2).astype(jnp.int32)
        for lane in range(2):
            at = jnp.where(own_z >= 2, 2, 0) + lane
            for half in range(2):
                start = pl.multiple_of(right * 256 + half * 128, 128)
                lead[at, :, pl.ds(start, 128)] = leads[k][lane * 2 + half]

    for j in range(2):
        change = mul3(
            rh[0:2].reshape(512, 1024), rl[0:2].reshape(512, 1024), eh[j], el[j]
        )
        for i in range(2):
            listed = child_mask[0, (p + 2 * i) * 8 + q, j] == 1
            part = change[i * 256 : i * 256 + 256]
            lead[i, :, j * 256 : j * 256 + 256] -= jnp.where(listed, part, 0.0)

    for pair in range(2):
        ah, al = halves(lead[2 * pair : 2 * pair + 2].reshape(512, 512))
        left = mul3(ah[:, :256], al[:, :256], vh[:256, :256], vl[:256, :256])
        right = mul3(ah, al, vh[256:, :], vl[256:, :])
        for half, value in enumerate((left, right)):
            a, b = halves(value)
            cols = slice(half * 256, half * 256 + 256)
            for i in range(2):
                rows = slice(i * 256, i * 256 + 256)
                panel[2 * pair + i, :, cols] = value[rows]
                ph[2 * pair + i, :, cols] = a[rows]
                pll[2 * pair + i, :, cols] = b[rows]
                for n in range(2):
                    to_send[2 * pair + i, 2 * half + n] = value[rows, n * 128 : n * 128 + 128]


def rows_step(spot, child_mask, inv, gathered, leads, edge_twin):
    f32, bf16 = jnp.float32, jnp.bfloat16
    vmem = pl.BlockSpec(memory_space=pltpu.VMEM)
    smem = pl.BlockSpec(memory_space=pltpu.SMEM)
    return pl.pallas_call(
        rows_kernel,
        out_shape=(
            jax.ShapeDtypeStruct((4, BS, 512), f32),
            jax.ShapeDtypeStruct((4, 4, BS, 128), f32),
            jax.ShapeDtypeStruct((4, BS, 1024), bf16),
            jax.ShapeDtypeStruct((4, BS, 1024), bf16),
            jax.ShapeDtypeStruct((4, BS, 512), bf16),
            jax.ShapeDtypeStruct((4, BS, 512), bf16),
        ),
        in_specs=[smem, smem, vmem] + [pl.BlockSpec(memory_space=pltpu.HBM)] * 9,
        out_specs=[vmem] * 6,
        scratch_shapes=[
            pltpu.VMEM((2, BS, 1024), bf16),
            pltpu.VMEM((2, BS, 1024), bf16),
            pltpu.VMEM((4, BS, 512), f32),
            pltpu.VMEM((512, 512), bf16),
            pltpu.VMEM((512, 512), bf16),
            pltpu.VMEM((4, 8, BS, 128), f32),
            pltpu.VMEM((4, 6, BS, 128), f32),
            pltpu.VMEM((8, BS, 128), f32),
            pltpu.SemaphoreType.DMA((9,)),
        ],
        compiler_params=pltpu.CompilerParams(vmem_limit_bytes=60 * 1024 * 1024),
        cost_estimate=pl.CostEstimate(flops=4_000_000_000, bytes_accessed=18_000_000, transcendentals=0),
        name="rows",
    )(spot, child_mask, inv, *gathered, *leads, edge_twin)


def update_kernel(spot, child_mask, parent, rh, rl, *refs):
    arrays, (out, ch, cl, acc) = refs[:8], refs[8:]
    p, x, core, yhi, z = (spot[n] for n in range(5))
    q = 2 * x + core
    c = 4 * yhi + z
    slot = pl.program_id(0)

    @pl.when(slot == 0)
    def _():
        for n in range(8):
            lane = core if n < 4 else 1 - core
            z_from = lax.rem(z + x + (0, 1, 3, 2)[n % 4] - (2 * yhi + z // 2) + 4, 4)
            for part in range(2):
                plane = p if part == 0 else 1 - p
                child = lax.rem(plane + lane, 2)
                for yr in range(2):
                    start = pl.multiple_of(z_from * 256 + lax.rem(yhi + yr, 2) * 128, 128)
                    for i in range(2):
                        a, b = halves(arrays[n][part * 4 + yr * 2 + i])
                        ch[child * 4 + plane + 2 * i, :, pl.ds(start, 128)] = a
                        cl[child * 4 + plane + 2 * i, :, pl.ds(start, 128)] = b

    for j in range(8):
        touched = j < 6
        for half in range(2):
            at = pl.ds(2 * j + half, BS, stride=16)
            if touched:
                acc[:, half * 128 : half * 128 + 128] = parent[at, :]
            else:
                out[at, :] = parent[at, :]
        if not touched:
            continue
        for child in range(2):
            s = j - 2 * child
            if s < 0 or s >= 4:
                continue
            i = jnp.clip(slot - child, 0, 1)
            listed = child_mask[child, (p + 2 * i) * 8 + q, s * 8 + c] == 1

            @pl.when(jnp.logical_and(listed, slot - child == i))
            def _():
                acc[...] -= mul3(
                    rh[child * 2 + i], rl[child * 2 + i], ch[child * 4 + s], cl[child * 4 + s]
                )

        for half in range(2):
            out[pl.ds(2 * j + half, BS, stride=16), :] = acc[:, half * 128 : half * 128 + 128]


def update_step(spot, child_mask, flat, rh, rl, arrays):
    vmem = pl.BlockSpec(memory_space=pltpu.VMEM)
    smem = pl.BlockSpec(memory_space=pltpu.SMEM)
    block = pl.BlockSpec((BS * 16, 128), lambda i: (i, 0))
    return pl.pallas_call(
        update_kernel,
        grid=(4,),
        out_shape=jax.ShapeDtypeStruct(flat.shape, jnp.float32),
        in_specs=[smem, smem, block] + [vmem] * (2 + len(arrays)),
        out_specs=block,
        scratch_shapes=[
            pltpu.VMEM((8, BS, 1024), jnp.bfloat16),
            pltpu.VMEM((8, BS, 1024), jnp.bfloat16),
            pltpu.VMEM((BS, BS), jnp.float32),
        ],
        compiler_params=pltpu.CompilerParams(vmem_limit_bytes=40 * 1024 * 1024),
        cost_estimate=pl.CostEstimate(flops=6_400_000_000, bytes_accessed=28_000_000, transcendentals=0),
        name="update",
    )(spot, child_mask, flat, rh, rl, *arrays)


def trail_kernel(spot, panel_mask, assembled, ph, pll, *refs):
    arrays, (out, qh, ql) = refs[:8], refs[8:]
    p, x, core, yhi, z = (spot[n] for n in range(5))
    r = 8 * p + 2 * x + core
    c = 4 * yhi + z
    right, slot = pl.program_id(0), pl.program_id(1)

    @pl.when(jnp.logical_and(right == 0, slot == 0))
    def _():
        for n in range(8):
            lane = core if n < 4 else 1 - core
            from_slot = lax.rem(x + (0, 1, 3, 2)[n % 4] - (2 * yhi + z // 2) + 4, 4)
            for part in range(2):
                plane = p if part == 0 else 1 - p
                for half in range(2):
                    start = pl.multiple_of(lane * 256 + half * 128, 128)
                    a, b = halves(arrays[n][part * 2 + half])
                    qh[plane * 4 + from_slot, :, pl.ds(start, 128)] = a
                    ql[plane * 4 + from_slot, :, pl.ds(start, 128)] = b

    row_block = 16 * slot + r
    for jj in range(4):
        j = 4 * right + jj
        col_block = 8 * j + c
        n = lax.rem(j, 2) * 4 + j // 2
        use = jnp.logical_and(row_block >= 2, col_block >= 2)
        use = jnp.logical_and(use, panel_mask[row_block, col_block] == 1)

        @pl.when(use)
        def _():
            product = mul3(ph[slot], pll[slot], qh[n], ql[n])
            for half in range(2):
                out[:, 2 * jj + half, :] = (
                    assembled[:, 2 * jj + half, :] - product[:, half * 128 : half * 128 + 128]
                )

        @pl.when(jnp.logical_not(use))
        def _():
            for half in range(2):
                out[:, 2 * jj + half, :] = assembled[:, 2 * jj + half, :]


def trail_step(spot, panel_mask, assembled, ph, pll, arrays):
    vmem = pl.BlockSpec(memory_space=pltpu.VMEM)
    smem = pl.BlockSpec(memory_space=pltpu.SMEM)
    block = pl.BlockSpec((BS, 8, 128), lambda j, i: (i, j, 0))
    return pl.pallas_call(
        trail_kernel,
        grid=(2, 4),
        out_shape=jax.ShapeDtypeStruct((4 * BS, 16, 128), jnp.float32),
        in_specs=[smem, smem, block] + [vmem] * (2 + len(arrays)),
        out_specs=block,
        scratch_shapes=[
            pltpu.VMEM((8, BS, 512), jnp.bfloat16),
            pltpu.VMEM((8, BS, 512), jnp.bfloat16),
        ],
        compiler_params=pltpu.CompilerParams(vmem_limit_bytes=40 * 1024 * 1024),
        cost_estimate=pl.CostEstimate(flops=6_400_000_000, bytes_accessed=22_000_000, transcendentals=0),
        name="trail",
    )(spot, panel_mask, assembled, ph, pll, *arrays)


def gate_kernel(*refs):
    pass


def gate(values, after, kind=pltpu.HBM, room=60):
    far = pl.BlockSpec(memory_space=kind)
    return pl.pallas_call(
        gate_kernel,
        out_shape=[jax.ShapeDtypeStruct(v.shape, v.dtype) for v in values],
        in_specs=[far] * (len(values) + len(after)),
        out_specs=[far] * len(values),
        input_output_aliases={i: i for i in range(len(values))},
        compiler_params=pltpu.CompilerParams(vmem_limit_bytes=room * 1024 * 1024),
        cost_estimate=pl.CostEstimate(flops=0, bytes_accessed=0, transcendentals=0),
        name="gate",
    )(*values, *after)


def shards(child_factor, parent, row_map, child_listed, inv_diag, panel_listed):
    p, x, core, yhi, z = (lax.axis_index(a) for a in AXES)
    spot = jnp.stack([p, x, core, yhi, z]).astype(jnp.int32)
    q = 2 * x + core
    first = core == 0
    own = child_factor.reshape(4, BS, 128)
    own_map = lax.dynamic_slice(row_map.reshape(2, 4, 8, BS), (p, 0, q, 0), (1, 4, 1, BS)).reshape(4, BS)
    placed, nothing = place(spot[:1], own, own_map)
    mine, other = placed[0], placed[1]

    late = parent.reshape(4, BS, 16, 128)[:, :, :2, :].transpose(0, 2, 1, 3) + nothing[0, 0]
    flat = parent.reshape(4 * BS * 16, 128)

    edges = lax.all_gather(lax.all_gather(mine[0], "x")[0], ("ylo", "yhi"))[:2]
    edge = jnp.where(yhi == 0, edges, edges[::-1])
    near = send(mine, route(lambda d: {"yhi": 1 - d["yhi"]}))
    cross = send(other, route(lambda d: {"ylo": 1 - d["ylo"]}))
    cross_far = send(other, route(lambda d: {"ylo": 1 - d["ylo"], "yhi": 1 - d["yhi"]}))
    spread = send(late[2:], route(lambda d: {"z": 3 - d["z"]}, lambda d: d["yhi"] == 0 and d["z"] < 2))
    near, cross, cross_far, spread = gate([near, cross, cross_far, spread], [])

    block = jnp.concatenate([mine, near, cross, cross_far])
    lead_piece = jnp.where(z < 2, late[:2], spread)
    ring = route(lambda d: {"z": d["z"] + (1 if d["core"] == 0 else -1)})
    twin = route(lambda d: {"core": 1 - d["core"]})
    swap = route(lambda d: {"ylo": 1 - d["ylo"]})
    around = [route(lambda d: {"x": d["x"] - n}) for n in (1, 3, 2)]

    def target(lane, cross=False):
        def move(d):
            z_to = 2 * (d["x"] % 2) + d["core"]
            plane = d["ylo"] + 1 if cross else d["ylo"]
            return {"ylo": plane, "x": d["x"] + d["z"] - z_to, "z": z_to, "core": lane}

        return route(move, lambda d: d["yhi"] == d["x"] // 2)

    def scatter(parts, cross=False):
        return [send(part, target(lane, cross)) for lane, part in enumerate(parts)]

    gathered = [block]
    arrived = send(block, ring)
    spread = send(lead_piece, route(lambda d: {"yhi": 1}, lambda d: d["yhi"] == 0))
    pieces = scatter([block[:4], block[4:]])
    arrived, spread, *pieces = gate([arrived, spread] + pieces, [])
    gathered.append(arrived)
    lead_piece = jnp.where(yhi == 0, lead_piece, spread).reshape(4, BS, 128)
    leads = [jnp.concatenate([lead_piece, edge])]
    quarter = jnp.where(first, pieces[0], pieces[1])

    arrived = send(gathered[-1], ring)
    lead_next = send(leads[-1], ring)
    other_quarter = send(quarter, swap)
    arrived, lead_next, other_quarter = gate([arrived, lead_next, other_quarter], [])
    gathered.append(arrived)
    leads.append(lead_next)

    columns = [jnp.concatenate([quarter, other_quarter])]
    arrived = send(gathered[-1], ring)
    lead_next = send(leads[-1], ring)
    moving = [send(columns[0], pairs) for pairs in around[:2]]
    arrived, lead_next, *moving = gate([arrived, lead_next] + moving, [])
    gathered.append(arrived)
    leads.append(lead_next)
    columns += moving
    onward = route(lambda d: {"x": d["x"] + (1 if d["core"] == 0 else -1)})
    lead_next = send(leads[-1], ring)
    relayed = send(jnp.where(first, columns[2], columns[1]), onward)
    arrays = [send(value, twin) for value in columns]
    lead_next, relayed, *arrays = gate([lead_next, relayed] + arrays, [])
    leads.append(lead_next)
    columns.append(relayed)

    edge_own = jnp.concatenate([block[4:] for block in leads])
    edge_twin = send(edge_own, twin)
    panel, to_send, rh, rl, ph, pll = rows_step(
        spot, child_listed, inv_diag, gathered, leads, edge_twin
    )
    turn = (z - (2 * (x % 2) + core)) % 4
    mine = lax.dynamic_index_in_dim(to_send, turn, 0, keepdims=False)
    pieces = gate(scatter([mine[:2], mine[2:]]), [], pl.ANY, 1)
    quarter = jnp.where(first, pieces[0], pieces[1])
    arrays.append(send(columns[3], twin))
    other_quarter, arrays[3] = gate([send(quarter, swap), arrays[3]], [], pl.ANY, 1)
    panels = [jnp.concatenate([quarter, other_quarter])]
    panels += [send(panels[0], pairs) for pairs in around]
    assembled = update_step(spot, child_listed, flat, rh, rl, columns + arrays)
    twins = [send(panels[0], twin)]
    (assembled,) = gate([assembled], [])
    panels[1:] = gate(panels[1:], [assembled], pl.ANY, 1)
    panels += twins + [send(value, twin) for value in panels[1:]]
    factored = trail_step(
        spot, panel_listed, assembled.reshape(4 * BS, 16, 128), ph, pll, panels
    )
    return factored.reshape(parent.shape), panel.reshape(4, 1, BS, 512)


def solution(mesh):
    grid = Mesh(mesh.devices.reshape(SIZES), AXES)
    row, col = ("ylo", "x", "core"), ("yhi", "z")
    return jax.shard_map(
        shards,
        mesh=grid,
        in_specs=(
            P(None, row, None, col),
            P(None, row, None, None, col, None),
            P(),
            P(),
            P(),
            P(),
        ),
        out_specs=(P(None, row, None, None, col, None), P(None, row, None, None)),
        check_vma=False,
    )
```

```python
import functools
import itertools
import jax
import jax.numpy as jnp
from jax import lax
from jax.experimental import pallas as pl
from jax.experimental.pallas import tpu as pltpu
from jax.sharding import Mesh, PartitionSpec as P

BS = 256
AXES = ("ylo", "x", "core", "yhi", "z")
SIZES = (2, 4, 2, 2, 4)
NT = (((1,), (1,)), ((), ()))


def route(move, keep=lambda dev: True):
    pairs = []
    for spot in itertools.product(*[range(n) for n in SIZES]):
        dev = dict(zip(AXES, spot))
        if not keep(dev):
            continue
        far = dict(dev)
        far.update(move(dev))
        flat = []
        for d in (dev, far):
            i = 0
            for a, n in zip(AXES, SIZES):
                i = i * n + d[a] % n
            flat.append(i)
        pairs.append(tuple(flat))
    return pairs


def send(value, pairs):
    return lax.ppermute(value, AXES, pairs)


def home(dev):
    return 2 * dev["yhi"] + dev["z"] // 2


def away(dev):
    apart = dev["x"] - home(dev)
    return (apart if dev["core"] == 0 else -apart) % 4


def halves(value):
    high = value.astype(jnp.bfloat16)
    return high, (value - high.astype(jnp.float32)).astype(jnp.bfloat16)


def mul3(ah, al, bh, bl):
    def dot(u, v):
        return lax.dot_general(u, v, NT, preferred_element_type=jnp.float32)

    return dot(ah, bh) + (dot(ah, bl) + dot(al, bh))


def place_kernel(where, own, maps, out, token):
    half = where[0]
    token[...] = jnp.zeros_like(token)
    for s in range(4):
        spots = lax.broadcasted_iota(jnp.int32, (BS, BS), 0)
        pick = jnp.where(spots == maps[s, :][None, :], 1.0, 0.0).astype(jnp.bfloat16)
        value = own[s]
        total = None
        for _ in range(3):
            part = value.astype(jnp.bfloat16)
            value = value - part.astype(jnp.float32)
            moved = jnp.dot(pick, part, preferred_element_type=jnp.float32)
            total = moved if total is None else total + moved
        out[lax.rem(half + s, 2), s // 2] = total


def place(half, own, maps):
    return pl.pallas_call(
        place_kernel,
        out_shape=(
            jax.ShapeDtypeStruct((2, 2, BS, 128), jnp.float32),
            jax.ShapeDtypeStruct((8, 128), jnp.float32),
        ),
        in_specs=[
            pl.BlockSpec(memory_space=pltpu.SMEM),
            pl.BlockSpec(memory_space=pltpu.VMEM),
            pl.BlockSpec(memory_space=pltpu.VMEM),
        ],
        out_specs=[pl.BlockSpec(memory_space=pltpu.VMEM)] * 2,
        name="place",
    )(half, own, maps)


def rows_kernel(spot, child_mask, inv, *refs):
    sources = refs[0:9]
    panel, to_send, rh, rl, ph, pll = refs[9:15]
    eh, el, lead, vh, vl, held, held_leads, edge_twin, sems = refs[15:]
    gathered = [held.at[k] for k in range(4)]
    leads = [held_leads.at[k] for k in range(4)]
    copies = [
        pltpu.make_async_copy(source, spot_of, sems.at[n])
        for n, (source, spot_of) in enumerate(zip(sources, gathered + leads + [edge_twin]))
    ]
    for n in (0, 4, 8, 1, 5, 2, 6, 3, 7):
        copies[n].start()
    p, x, core, yhi, z = (spot[n] for n in range(5))
    q = 2 * x + core
    turn = jnp.where(core == 0, 1, 3)

    a, b = halves(inv[...])
    vh[...] = a
    vl[...] = b
    copies[8].wait()
    for k in range(4):
        copies[k].wait()
        copies[4 + k].wait()
        own_z = lax.rem(z + 16 - turn * k, 4)
        twin_z = lax.rem(z + turn * k, 4)
        for yr in range(2):
            y_at = lax.rem(yhi + yr, 2)
            start = pl.multiple_of(own_z * 256 + y_at * 128, 128)
            for lane in range(2):
                child = lax.rem(p + lane, 2)
                for i in range(2):
                    a, b = halves(gathered[k][lane * 4 + yr * 2 + i])
                    rh[child * 2 + i, :, pl.ds(start, 128)] = a
                    rl[child * 2 + i, :, pl.ds(start, 128)] = b
            a, b = halves(leads[k][4 + yr])
            eh[core, :, pl.ds(start, 128)] = a
            el[core, :, pl.ds(start, 128)] = b
            start = pl.multiple_of(twin_z * 256 + y_at * 128, 128)
            a, b = halves(edge_twin[k * 2 + yr])
            eh[1 - core, :, pl.ds(start, 128)] = a
            el[1 - core, :, pl.ds(start, 128)] = b
        right = jnp.logical_or(own_z == 1, own_z == 2).astype(jnp.int32)
        for lane in range(2):
            at = jnp.where(own_z >= 2, 2, 0) + lane
            for half in range(2):
                start = pl.multiple_of(right * 256 + half * 128, 128)
                lead[at, :, pl.ds(start, 128)] = leads[k][lane * 2 + half]

    for j in range(2):
        change = mul3(
            rh[0:2].reshape(512, 1024), rl[0:2].reshape(512, 1024), eh[j], el[j]
        )
        for i in range(2):
            listed = child_mask[0, (p + 2 * i) * 8 + q, j] == 1
            part = change[i * 256 : i * 256 + 256]
            lead[i, :, j * 256 : j * 256 + 256] -= jnp.where(listed, part, 0.0)

    for pair in range(2):
        ah, al = halves(lead[2 * pair : 2 * pair + 2].reshape(512, 512))
        left = mul3(ah[:, :256], al[:, :256], vh[:256, :256], vl[:256, :256])
        right = mul3(ah, al, vh[256:, :], vl[256:, :])
        for half, value in enumerate((left, right)):
            a, b = halves(value)
            cols = slice(half * 256, half * 256 + 256)
            for i in range(2):
                rows = slice(i * 256, i * 256 + 256)
                panel[2 * pair + i, :, cols] = value[rows]
                ph[2 * pair + i, :, cols] = a[rows]
                pll[2 * pair + i, :, cols] = b[rows]
                for n in range(2):
                    to_send[2 * pair + i, 2 * half + n] = value[rows, n * 128 : n * 128 + 128]


def rows_step(spot, child_mask, inv, gathered, leads, edge_twin):
    f32, bf16 = jnp.float32, jnp.bfloat16
    vmem = pl.BlockSpec(memory_space=pltpu.VMEM)
    smem = pl.BlockSpec(memory_space=pltpu.SMEM)
    return pl.pallas_call(
        rows_kernel,
        out_shape=(
            jax.ShapeDtypeStruct((4, BS, 512), f32),
            jax.ShapeDtypeStruct((4, 4, BS, 128), f32),
            jax.ShapeDtypeStruct((4, BS, 1024), bf16),
            jax.ShapeDtypeStruct((4, BS, 1024), bf16),
            jax.ShapeDtypeStruct((4, BS, 512), bf16),
            jax.ShapeDtypeStruct((4, BS, 512), bf16),
        ),
        in_specs=[smem, smem, vmem] + [pl.BlockSpec(memory_space=pltpu.HBM)] * 9,
        out_specs=[vmem] * 6,
        scratch_shapes=[
            pltpu.VMEM((2, BS, 1024), bf16),
            pltpu.VMEM((2, BS, 1024), bf16),
            pltpu.VMEM((4, BS, 512), f32),
            pltpu.VMEM((512, 512), bf16),
            pltpu.VMEM((512, 512), bf16),
            pltpu.VMEM((4, 8, BS, 128), f32),
            pltpu.VMEM((4, 6, BS, 128), f32),
            pltpu.VMEM((8, BS, 128), f32),
            pltpu.SemaphoreType.DMA((9,)),
        ],
        compiler_params=pltpu.CompilerParams(vmem_limit_bytes=60 * 1024 * 1024),
        cost_estimate=pl.CostEstimate(flops=4_000_000_000, bytes_accessed=18_000_000, transcendentals=0),
        name="rows",
    )(spot, child_mask, inv, *gathered, *leads, edge_twin)


def split_kernel(spot, *refs):
    arrays, (ch, cl) = refs[:8], refs[8:]
    p, x, core, yhi, z = (spot[n] for n in range(5))
    for n in range(8):
        lane = core if n < 4 else 1 - core
        z_from = lax.rem(z + x + (0, 1, 3, 2)[n % 4] - (2 * yhi + z // 2) + 4, 4)
        for part in range(2):
            plane = p if part == 0 else 1 - p
            child = lax.rem(plane + lane, 2)
            for yr in range(2):
                start = pl.multiple_of(z_from * 256 + lax.rem(yhi + yr, 2) * 128, 128)
                for i in range(2):
                    a, b = halves(arrays[n][part * 4 + yr * 2 + i])
                    ch[child * 4 + plane + 2 * i, :, pl.ds(start, 128)] = a
                    cl[child * 4 + plane + 2 * i, :, pl.ds(start, 128)] = b


def split_step(spot, arrays):
    vmem = pl.BlockSpec(memory_space=pltpu.VMEM)
    return pl.pallas_call(
        split_kernel,
        out_shape=[jax.ShapeDtypeStruct((8, BS, 1024), jnp.bfloat16)] * 2,
        in_specs=[pl.BlockSpec(memory_space=pltpu.SMEM)] + [vmem] * 8,
        out_specs=[vmem] * 2,
        compiler_params=pltpu.CompilerParams(vmem_limit_bytes=40 * 1024 * 1024),
        cost_estimate=pl.CostEstimate(flops=0, bytes_accessed=16_000_000, transcendentals=0),
        name="split",
    )(spot, *arrays)


def update_kernel(spot, child_mask, parent, rh, rl, ch, cl, out, acc):
    p, x, core, yhi, z = (spot[n] for n in range(5))
    q = 2 * x + core
    c = 4 * yhi + z
    slot = pl.program_id(0)

    for j in range(8):
        touched = j < 6
        for half in range(2):
            at = pl.ds(2 * j + half, BS, stride=16)
            if touched:
                acc[:, half * 128 : half * 128 + 128] = parent[at, :]
            else:
                out[at, :] = parent[at, :]
        if not touched:
            continue
        for child in range(2):
            s = j - 2 * child
            if s < 0 or s >= 4:
                continue
            i = jnp.clip(slot - child, 0, 1)
            listed = child_mask[child, (p + 2 * i) * 8 + q, s * 8 + c] == 1

            @pl.when(jnp.logical_and(listed, slot - child == i))
            def _():
                acc[...] -= mul3(
                    rh[child * 2 + i], rl[child * 2 + i], ch[child * 4 + s], cl[child * 4 + s]
                )

        for half in range(2):
            out[pl.ds(2 * j + half, BS, stride=16), :] = acc[:, half * 128 : half * 128 + 128]


def update_step(spot, child_mask, flat, rh, rl, arrays):
    vmem = pl.BlockSpec(memory_space=pltpu.VMEM)
    smem = pl.BlockSpec(memory_space=pltpu.SMEM)
    block = pl.BlockSpec((BS * 16, 128), lambda i: (i, 0))
    return pl.pallas_call(
        update_kernel,
        grid=(4,),
        out_shape=jax.ShapeDtypeStruct(flat.shape, jnp.float32),
        in_specs=[smem, smem, block] + [vmem] * (2 + len(arrays)),
        out_specs=block,
        scratch_shapes=[
            pltpu.VMEM((BS, BS), jnp.float32),
        ],
        compiler_params=pltpu.CompilerParams(vmem_limit_bytes=40 * 1024 * 1024),
        cost_estimate=pl.CostEstimate(flops=6_400_000_000, bytes_accessed=28_000_000, transcendentals=0),
        name="update",
    )(spot, child_mask, flat, rh, rl, *arrays)


def trail_kernel(spot, panel_mask, assembled, ph, pll, *refs):
    arrays, (out, qh, ql) = refs[:8], refs[8:]
    p, x, core, yhi, z = (spot[n] for n in range(5))
    r = 8 * p + 2 * x + core
    c = 4 * yhi + z
    right, slot = pl.program_id(0), pl.program_id(1)

    @pl.when(jnp.logical_and(right == 0, slot == 0))
    def _():
        for n in range(8):
            lane = core if n < 4 else 1 - core
            from_slot = lax.rem(x + (0, 1, 3, 2)[n % 4] - (2 * yhi + z // 2) + 4, 4)
            for part in range(2):
                plane = p if part == 0 else 1 - p
                for half in range(2):
                    start = pl.multiple_of(lane * 256 + half * 128, 128)
                    a, b = halves(arrays[n][part * 2 + half])
                    qh[plane * 4 + from_slot, :, pl.ds(start, 128)] = a
                    ql[plane * 4 + from_slot, :, pl.ds(start, 128)] = b

    row_block = 16 * slot + r
    for jj in range(4):
        j = 4 * right + jj
        col_block = 8 * j + c
        n = lax.rem(j, 2) * 4 + j // 2
        use = jnp.logical_and(row_block >= 2, col_block >= 2)
        use = jnp.logical_and(use, panel_mask[row_block, col_block] == 1)

        @pl.when(use)
        def _():
            product = mul3(ph[slot], pll[slot], qh[n], ql[n])
            for half in range(2):
                out[:, 2 * jj + half, :] = (
                    assembled[:, 2 * jj + half, :] - product[:, half * 128 : half * 128 + 128]
                )

        @pl.when(jnp.logical_not(use))
        def _():
            for half in range(2):
                out[:, 2 * jj + half, :] = assembled[:, 2 * jj + half, :]


def trail_step(spot, panel_mask, assembled, ph, pll, arrays):
    vmem = pl.BlockSpec(memory_space=pltpu.VMEM)
    smem = pl.BlockSpec(memory_space=pltpu.SMEM)
    block = pl.BlockSpec((BS, 8, 128), lambda j, i: (i, j, 0))
    return pl.pallas_call(
        trail_kernel,
        grid=(2, 4),
        out_shape=jax.ShapeDtypeStruct((4 * BS, 16, 128), jnp.float32),
        in_specs=[smem, smem, block] + [vmem] * (2 + len(arrays)),
        out_specs=block,
        scratch_shapes=[
            pltpu.VMEM((8, BS, 512), jnp.bfloat16),
            pltpu.VMEM((8, BS, 512), jnp.bfloat16),
        ],
        compiler_params=pltpu.CompilerParams(vmem_limit_bytes=40 * 1024 * 1024),
        cost_estimate=pl.CostEstimate(flops=6_400_000_000, bytes_accessed=22_000_000, transcendentals=0),
        name="trail",
    )(spot, panel_mask, assembled, ph, pll, *arrays)


def gate_kernel(*refs):
    pass


def gate(values, after, kind=pltpu.HBM, room=60):
    far = pl.BlockSpec(memory_space=kind)
    return pl.pallas_call(
        gate_kernel,
        out_shape=[jax.ShapeDtypeStruct(v.shape, v.dtype) for v in values],
        in_specs=[far] * (len(values) + len(after)),
        out_specs=[far] * len(values),
        input_output_aliases={i: i for i in range(len(values))},
        compiler_params=pltpu.CompilerParams(vmem_limit_bytes=room * 1024 * 1024),
        cost_estimate=pl.CostEstimate(flops=0, bytes_accessed=0, transcendentals=0),
        name="gate",
    )(*values, *after)


def shards(child_factor, parent, row_map, child_listed, inv_diag, panel_listed):
    p, x, core, yhi, z = (lax.axis_index(a) for a in AXES)
    spot = jnp.stack([p, x, core, yhi, z]).astype(jnp.int32)
    q = 2 * x + core
    first = core == 0
    own = child_factor.reshape(4, BS, 128)
    own_map = lax.dynamic_slice(row_map.reshape(2, 4, 8, BS), (p, 0, q, 0), (1, 4, 1, BS)).reshape(4, BS)
    placed, nothing = place(spot[:1], own, own_map)
    mine, other = placed[0], placed[1]

    late = parent.reshape(4, BS, 16, 128)[:, :, :2, :].transpose(0, 2, 1, 3) + nothing[0, 0]
    flat = parent.reshape(4 * BS * 16, 128)

    edges = lax.all_gather(lax.all_gather(mine[0], "x")[0], ("ylo", "yhi"))[:2]
    edge = jnp.where(yhi == 0, edges, edges[::-1])
    near = send(mine, route(lambda d: {"yhi": 1 - d["yhi"]}))
    cross = send(other, route(lambda d: {"ylo": 1 - d["ylo"]}))
    cross_far = send(other, route(lambda d: {"ylo": 1 - d["ylo"], "yhi": 1 - d["yhi"]}))
    spread = send(late[2:], route(lambda d: {"z": 3 - d["z"]}, lambda d: d["yhi"] == 0 and d["z"] < 2))
    near, cross, cross_far, spread = gate([near, cross, cross_far, spread], [])

    block = jnp.concatenate([mine, near, cross, cross_far])
    lead_piece = jnp.where(z < 2, late[:2], spread)
    ring = route(lambda d: {"z": d["z"] + (1 if d["core"] == 0 else -1)})
    twin = route(lambda d: {"core": 1 - d["core"]})
    swap = route(lambda d: {"ylo": 1 - d["ylo"]})
    around = [route(lambda d: {"x": d["x"] - n}) for n in (1, 3, 2)]

    def target(lane, cross=False):
        def move(d):
            z_to = 2 * (d["x"] % 2) + d["core"]
            plane = d["ylo"] + 1 if cross else d["ylo"]
            return {"ylo": plane, "x": d["x"] + d["z"] - z_to, "z": z_to, "core": lane}

        return route(move, lambda d: d["yhi"] == d["x"] // 2)

    def scatter(parts, cross=False):
        return [send(part, target(lane, cross)) for lane, part in enumerate(parts)]

    gathered = [block]
    arrived = send(block, ring)
    spread = send(lead_piece, route(lambda d: {"yhi": 1}, lambda d: d["yhi"] == 0))
    pieces = scatter([block[:4], block[4:]])
    arrived, spread, *pieces = gate([arrived, spread] + pieces, [])
    gathered.append(arrived)
    lead_piece = jnp.where(yhi == 0, lead_piece, spread).reshape(4, BS, 128)
    leads = [jnp.concatenate([lead_piece, edge])]
    quarter = jnp.where(first, pieces[0], pieces[1])

    arrived = send(gathered[-1], ring)
    lead_next = send(leads[-1], ring)
    other_quarter = send(quarter, swap)
    arrived, lead_next, other_quarter = gate([arrived, lead_next, other_quarter], [])
    gathered.append(arrived)
    leads.append(lead_next)

    columns = [jnp.concatenate([quarter, other_quarter])]
    arrived = send(gathered[-1], ring)
    lead_next = send(leads[-1], ring)
    moving = [send(columns[0], pairs) for pairs in around[:2]]
    arrived, lead_next, *moving = gate([arrived, lead_next] + moving, [])
    gathered.append(arrived)
    leads.append(lead_next)
    columns += moving
    onward = route(lambda d: {"x": d["x"] + (1 if d["core"] == 0 else -1)})
    lead_next = send(leads[-1], ring)
    relayed = send(jnp.where(first, columns[2], columns[1]), onward)
    arrays = [send(value, twin) for value in columns]
    lead_next, relayed, *arrays = gate([lead_next, relayed] + arrays, [])
    leads.append(lead_next)
    columns.append(relayed)

    edge_own = jnp.concatenate([block[4:] for block in leads])
    edge_twin, last = gate([send(edge_own, twin), send(columns[3], twin)], [])
    arrays.append(last)
    panel, to_send, rh, rl, ph, pll = rows_step(
        spot, child_listed, inv_diag, gathered, leads, edge_twin
    )
    turn = (z - (2 * (x % 2) + core)) % 4
    mine = lax.dynamic_index_in_dim(to_send, turn, 0, keepdims=False)
    pieces = scatter([mine[:2], mine[2:]])
    split = list(split_step(spot, columns + arrays))
    pieces = gate(pieces, split, pl.ANY, 1)
    quarter = jnp.where(first, pieces[0], pieces[1])
    (other_quarter,) = gate([send(quarter, swap)], [], pl.ANY, 1)
    panels = [jnp.concatenate([quarter, other_quarter])]
    panels += [send(panels[0], pairs) for pairs in around]
    assembled = update_step(spot, child_listed, flat, rh, rl, split)
    twins = [send(panels[0], twin)]
    (assembled,) = gate([assembled], [])
    panels[1:] = gate(panels[1:], [assembled], pl.ANY, 1)
    panels += twins + [send(value, twin) for value in panels[1:]]
    factored = trail_step(
        spot, panel_listed, assembled.reshape(4 * BS, 16, 128), ph, pll, panels
    )
    return factored.reshape(parent.shape), panel.reshape(4, 1, BS, 512)


def solution(mesh):
    grid = Mesh(mesh.devices.reshape(SIZES), AXES)
    row, col = ("ylo", "x", "core"), ("yhi", "z")
    return jax.shard_map(
        shards,
        mesh=grid,
        in_specs=(
            P(None, row, None, col),
            P(None, row, None, None, col, None),
            P(),
            P(),
            P(),
            P(),
        ),
        out_specs=(P(None, row, None, None, col, None), P(None, row, None, None)),
        check_vma=False,
    )
```
